32 devices in a mesh: silo: 8 (over y, x, core), fsdp: 4 (over z).
Axes of the slice: x: 2, y: 2, z: 4, core: 2. Of those that a mesh axis runs over, the one named last changes fastest.
Arguments:
- activations: bfloat16 [8, 1024, 2304], P('silo', 'fsdp'), may hold values from -6 to 6
- key_cot: bfloat16 [8, 1024, 512], P('silo', 'fsdp'), may hold values from -0.29882812 to 0.29882812
- key_weight: bfloat16 [8, 2304, 512], P('silo', 'fsdp'), may hold values from -0.125 to 0.125
- weight_first: float32 [8, 2304, 512], P('silo', 'fsdp'), may hold values from -2 to 2
- weight_second: float32 [8, 2304, 512], P('silo', 'fsdp'), may hold values from 1 to 16
- norm_gain: float32 [8, 2304], P('silo', 'fsdp'), may hold values from 0.5 to 1.5
- gain_first: float32 [8, 2304], P('silo', 'fsdp'), may hold values from -2 to 2
- gain_second: float32 [8, 2304], P('silo', 'fsdp'), may hold values from 0.5 to 4
- pseudo_grad: bfloat16 [8, 1572864], P('silo', 'fsdp'), may hold values from -6 to 6
- outer_params: float32 [1572864], P('fsdp'), may hold values from -6 to 6
- outer_mom: float32 [1572864], P('fsdp'), may hold values from -3 to 3
Outputs:
- keys: bfloat16 [8, 1024, 512], P('silo', 'fsdp')
- new_weight: bfloat16 [8, 2304, 512], P('silo', 'fsdp')
- new_weight_first: float32 [8, 2304, 512], P('silo', 'fsdp')
- new_weight_second: float32 [8, 2304, 512], P('silo', 'fsdp')
- new_gain: float32 [8, 2304], P('silo', 'fsdp')
- new_gain_first: float32 [8, 2304], P('silo', 'fsdp')
- new_gain_second: float32 [8, 2304], P('silo', 'fsdp')
- new_outer_params: float32 [1572864], P('fsdp')
- new_outer_mom: float32 [1572864], P('fsdp')
The draws below stay inside these ranges and needn't reach their ends.
All inputs are finite; a program needn't handle non-finite values.
Results may differ from the reference program's by a relative error of at most 0.0095.
Values may be sent and summed in bfloat16 or wider, within the bound.
No kernel may reach another device: no remote copies, remote signals or barrier semaphores. Data moves between devices by JAX's collectives and lax.ppermute only.
A program may use at most 64 MiB of HBM per device.

```python
import math
import jax
import jax.numpy as jnp
from jax import lax

FEAT = 2304
KVW = 512
TOK_DEV = 256
SILOS = 8
TOK_SILO = 1024
FRAG = 1572864
N_SILO = 8
N_FSDP = 4


def shard_levels(own_key, dims, shards, low, top_value):
    loudness, own = 1.0, jax.random.fold_in(own_key, 6)
    for dim, shards_of in shards:
        steps = jnp.exp(jax.random.uniform(jax.random.fold_in(own, dim), (shards_of,), jnp.float32, low / len(shards), top_value / len(shards)))
        loudness = loudness * jnp.repeat(steps, dims[dim] // shards_of).reshape([-1 if axis == dim else 1 for axis in range(len(dims))])
    return loudness


def bell_draw(key, shape, deviation, reach, split=(), kind=jnp.bfloat16):
    entries = jax.random.normal(key, shape, jnp.float32) * deviation
    if len(split) > 0:
        entries = shard_levels(key, shape, split, -0.22, 0.18) * entries
    return jnp.clip(entries, min=-reach, max=reach).astype(kind)


def setup_inputs(seed: int = 0) -> dict:
    streams_of = jax.random.split(jax.random.key(seed), 12)
    return {
        "activations": bell_draw(streams_of[0], (SILOS, TOK_SILO, FEAT), 1.0, 6.0, ((0, 8), (1, 4))),
        "key_cot": bell_draw(streams_of[1], (SILOS, TOK_SILO, KVW), 0.05, 0.29882812, ((0, 8), (1, 4))),
        "key_weight": bell_draw(streams_of[2], (SILOS, FEAT, KVW), FEAT ** -0.5, 0.125, ((0, 8), (1, 4))),
        "weight_first": bell_draw(streams_of[3], (SILOS, FEAT, KVW), 0.3, 2.0, ((0, 8), (1, 4)), jnp.float32),
        "weight_second": jnp.clip(jnp.exp(math.log(16.0) - 2.7725887 * jax.random.uniform(streams_of[4], (SILOS, FEAT, KVW), jnp.float32) ** shard_levels(streams_of[4], (SILOS, FEAT, KVW), ((0, 8), (1, 4)), -0.2, 0.2)), 1.0, 16.0),
        "norm_gain": jnp.clip(1.0 + 0.1 * jax.random.normal(streams_of[5], (SILOS, FEAT), jnp.float32), 0.5, 1.5),
        "gain_first": bell_draw(streams_of[6], (SILOS, FEAT), 0.3, 2.0, ((0, 8), (1, 4)), jnp.float32),
        "gain_second": jnp.clip(jnp.exp(math.log(4.0) - 2.0794415 * jax.random.uniform(streams_of[7], (SILOS, FEAT), jnp.float32) ** shard_levels(streams_of[7], (SILOS, FEAT), ((0, 8), (1, 4)), -0.2, 0.2)), 0.5, 4.0),
        "pseudo_grad": bell_draw(streams_of[8], (SILOS, FRAG), 1.0, 6.0, ((0, 8), (1, 4))),
        "outer_params": bell_draw(streams_of[9], (FRAG,), 1.0, 6.0, ((0, 4),), jnp.float32),
        "outer_mom": bell_draw(streams_of[10], (FRAG,), 0.5, 3.0, ((0, 4),), jnp.float32),
    }


norm_eps = 1e-05
beta_one = 0.9
beta_two = 0.95
corr_one = 1.0 - math.exp(200.0 * math.log(0.9))
corr_two = 1.0 - math.exp(200.0 * math.log(0.95))
learn_rate = 0.001
adam_eps = 1e-08
weight_decay = 0.1
outer_beta = 0.9
outer_rate = 0.7

def adam_step(params, gradient, first_moment, second_moment):
    first_new = beta_one * first_moment + (1.0 - beta_one) * gradient
    second_new = beta_two * second_moment + (1.0 - beta_two) * gradient * gradient
    update = first_new / corr_one / (jnp.sqrt(second_new / corr_two) + adam_eps) + weight_decay * params
    return (params - learn_rate * update, first_new, second_new)

def silo_step(silo_items):
    inputs, cotangent, weight, first_moment, second_moment, gain, gain_first, gain_second = silo_items
    wide_inputs = inputs.astype(jnp.float32)
    inv_rms = lax.rsqrt(lax.optimization_barrier(jnp.mean(wide_inputs * wide_inputs, axis=1, keepdims=True)) + norm_eps)
    gain_used = lax.optimization_barrier(gain.astype(jnp.bfloat16)).astype(jnp.float32)
    normed = (wide_inputs * inv_rms * gain_used[None, :]).astype(jnp.bfloat16)
    key_out = jnp.dot(normed, weight, preferred_element_type=jnp.float32).astype(jnp.bfloat16)
    back_grad = lax.dot_general(cotangent, weight, (((1,), (1,)), ((), ())), preferred_element_type=jnp.float32)
    gain_grad = lax.optimization_barrier(jnp.sum(back_grad * wide_inputs * inv_rms, axis=0))
    group_normed = normed.reshape(N_FSDP, TOK_DEV, FEAT).astype(jnp.float32)
    group_cot = cotangent.reshape(N_FSDP, TOK_DEV, KVW).astype(jnp.float32)
    partial_value = jnp.einsum('ntf,ntk->nfk', group_normed, group_cot)
    rounded = lax.optimization_barrier(partial_value.astype(jnp.bfloat16)).astype(jnp.float32)
    weight_grad = lax.optimization_barrier(jnp.sum(rounded, axis=0))
    new_weight, new_first, new_second = adam_step(weight.astype(jnp.float32), weight_grad, first_moment, second_moment)
    new_gain, new_gain_first, new_gain_second = adam_step(gain, gain_grad, gain_first, gain_second)
    return (key_out, new_weight.astype(jnp.bfloat16), new_first, new_second, new_gain, new_gain_first, new_gain_second)

def reference(activations, key_cot, key_weight, weight_first, weight_second, norm_gain, gain_first, gain_second, pseudo_grad, outer_params, outer_mom):
    results = lax.map(silo_step, (activations, key_cot, key_weight, weight_first, weight_second, norm_gain, gain_first, gain_second))
    silo_total = lax.optimization_barrier(jnp.sum(pseudo_grad, axis=0, dtype=jnp.float32))
    outer_delta = silo_total / N_SILO
    new_mom = outer_beta * outer_mom + outer_delta
    new_params = outer_params - outer_rate * (outer_delta + outer_beta * new_mom)
    return (results[0], results[1], results[2], results[3], results[4], results[5], results[6], new_params, new_mom)
```

```python
import math

import jax
import jax.numpy as jnp
from jax import lax
from jax.sharding import PartitionSpec as P

norm_eps = 1e-05
beta_one = 0.9
beta_two = 0.95
corr_one = 1.0 - math.exp(200.0 * math.log(0.9))
corr_two = 1.0 - math.exp(200.0 * math.log(0.95))
learn_rate = 0.001
adam_eps = 1e-08
weight_decay = 0.1
outer_beta = 0.9
outer_rate = 0.7
chunk_count = 2

wide = jnp.float32
narrow = jnp.bfloat16


def adam_step(params, gradient, first_moment, second_moment):
    first_new = beta_one * first_moment + (1.0 - beta_one) * gradient
    second_new = beta_two * second_moment + (1.0 - beta_two) * gradient * gradient
    update = (
        first_new / corr_one / (jnp.sqrt(second_new / corr_two) + adam_eps) + weight_decay * params
    )
    return (params - learn_rate * update, first_new, second_new)


def nesterov(delta_part, params_part, mom_part):
    new_mom = outer_beta * mom_part + delta_part
    new_params = params_part - outer_rate * (delta_part + outer_beta * new_mom)
    return (new_params, new_mom)


def add_narrow(left, right):
    return (left.astype(wide) + right.astype(wide)).astype(narrow)


def silo_sum(halves, silos):
    core = lax.axis_index("silo") & 1

    def swap(part, bit):
        return lax.ppermute(part, "silo", [(i, i ^ bit) for i in range(silos)])

    keep = lax.dynamic_index_in_dim(halves, core, 0, keepdims=False)
    give = lax.dynamic_index_in_dim(halves, 1 - core, 0, keepdims=False)
    total = add_narrow(keep, swap(give, 1))
    bit = 2
    while bit < silos:
        total = add_narrow(total, swap(total, bit))
        bit *= 2
    total = lax.optimization_barrier(total)
    other = swap(total, 1)
    first = jnp.where(core == 0, total, other)
    second = jnp.where(core == 0, other, total)
    return jnp.stack([first, second])


def outer_update(pseudo_grad, outer_params, outer_mom, silos):
    size = pseudo_grad.shape[1]
    spread = lax.optimization_barrier(pseudo_grad[0].astype(wide))
    if silos > 1 and silos & (silos - 1) == 0 and size % 4096 == 0:
        halves = spread.reshape(2, size // 256, 128).astype(narrow)
        total = silo_sum(halves, silos).astype(wide).reshape(size)
    else:
        total = lax.psum(spread, "silo")
    return nesterov(total / silos, outer_params, outer_mom)


def make(silos, n):
    def per_device(
        activations,
        key_cot,
        key_weight,
        weight_first,
        weight_second,
        norm_gain,
        gain_first,
        gain_second,
        pseudo_grad,
        outer_params,
        outer_mom,
    ):
        me = lax.axis_index("fsdp")
        inputs = activations[0]
        tokens, feats = inputs.shape
        rows, cols = key_weight.shape[1:]
        chunks = chunk_count if rows % (16 * chunk_count) == 0 else 1
        depth = rows // chunks

        wide_inputs = inputs.astype(wide)
        inv_rms = lax.rsqrt(
            jnp.mean(wide_inputs * wide_inputs, axis=1, keepdims=True) + norm_eps
        )
        cot_scaled = (key_cot[0].astype(wide) * inv_rms).astype(narrow)
        gain_used = norm_gain[0].astype(narrow).astype(wide)[:, None]
        weight = key_weight[0].astype(wide)
        weight_sent = (weight * gain_used).astype(narrow)

        partial = lax.dot_general(
            inputs, cot_scaled, (((0,), (0,)), ((), ())), preferred_element_type=wide
        ).astype(narrow)
        partial = partial.reshape(n, chunks, depth, cols)
        blocks = inputs.reshape(tokens, n, chunks, depth).transpose(1, 2, 0, 3)

        def shard_of(k, c):
            return lax.dynamic_index_in_dim(partial[:, c], k, 0, keepdims=False)

        def inputs_of(k, c):
            return lax.dynamic_index_in_dim(blocks[:, c], k, 0, keepdims=False)

        even = (me & 1) == 0
        links = [
            [pair for i in range(start, n - 1, 2) for pair in ((i, i + 1), (i + 1, i))]
            for start in (0, 1)
        ]
        to_right = [even, jnp.logical_not(even)]
        places = [jnp.where(right, me, n - 1 - me) for right in to_right]

        def device_at(k, right):
            k = jnp.clip(k, 0, n - 1)
            return jnp.where(right, k, n - 1 - k)

        own = weight_sent.reshape(chunks, depth, cols)
        acc = jnp.zeros((tokens, cols), wide)
        for c in range(chunks):
            acc = acc + jnp.dot(inputs_of(me, c), own[c], preferred_element_type=wide)
        got = [[None for _ in range(chunks)] for _ in links]
        for s in range(n):
            for c in range(chunks):
                sent = [own[c], own[c]]
                if s > 0:
                    for w in range(2):
                        before = got[1 - w][c]
                        owner = device_at(n - s + places[w], to_right[w])
                        sent[w] = jnp.where(
                            s > places[w], add_narrow(before, shard_of(owner, c)), before
                        )
                for w in range(2):
                    got[w][c] = lax.ppermute(sent[w], "fsdp", links[w])
            if s < n - 1:
                for c in range(chunks):
                    for w in range(2):
                        right, place = to_right[1 - w], places[1 - w]
                        block = inputs_of(device_at(place - 1 - s, right), c)
                        term = jnp.dot(block, got[w][c], preferred_element_type=wide)
                        acc = acc + jnp.where(s < place, term, 0.0)
        keys = (acc * inv_rms).astype(narrow)

        new_weight, new_first, new_second, gain_share = [], [], [], []
        for c in range(chunks):
            span = slice(c * depth, (c + 1) * depth)
            raw = shard_of(me, c).astype(wide)
            for w in range(2):
                raw = raw + got[w][c].astype(wide)
            gain_share.append(jnp.sum(raw * weight[span], axis=1))
            out = adam_step(
                weight[span], raw * gain_used[span], weight_first[0, span], weight_second[0, span]
            )
            new_weight.append(out[0].astype(narrow))
            new_first.append(out[1])
            new_second.append(out[2])
        new_gain, new_gain_first, new_gain_second = adam_step(
            norm_gain[0], jnp.concatenate(gain_share), gain_first[0], gain_second[0]
        )
        new_params, new_mom = outer_update(pseudo_grad, outer_params, outer_mom, silos)
        return (
            keys[None],
            jnp.concatenate(new_weight)[None],
            jnp.concatenate(new_first)[None],
            jnp.concatenate(new_second)[None],
            new_gain[None],
            new_gain_first[None],
            new_gain_second[None],
            new_params,
            new_mom,
        )

    return per_device


def solution(mesh):
    return jax.shard_map(
        make(mesh.shape["silo"], mesh.shape["fsdp"]),
        mesh=mesh,
        in_specs=(
            P("silo", "fsdp", None),
            P("silo", "fsdp", None),
            P("silo", "fsdp", None),
            P("silo", "fsdp", None),
            P("silo", "fsdp", None),
            P("silo", "fsdp"),
            P("silo", "fsdp"),
            P("silo", "fsdp"),
            P("silo", "fsdp"),
            P("fsdp"),
            P("fsdp"),
        ),
        out_specs=(
            P("silo", "fsdp", None),
            P("silo", "fsdp", None),
            P("silo", "fsdp", None),
            P("silo", "fsdp", None),
            P("silo", "fsdp"),
            P("silo", "fsdp"),
            P("silo", "fsdp"),
            P("fsdp"),
            P("fsdp"),
        ),
        check_vma=False,
    )
```

```python
import functools
import math

import jax
import jax.numpy as jnp
from jax import lax
from jax.experimental import pallas as pl
from jax.experimental.pallas import tpu as pltpu
from jax.sharding import PartitionSpec as P

norm_eps = 1e-05
beta_one = 0.9
beta_two = 0.95
corr_one = 1.0 - math.exp(200.0 * math.log(0.9))
corr_two = 1.0 - math.exp(200.0 * math.log(0.95))
learn_rate = 0.001
adam_eps = 1e-08
weight_decay = 0.1
outer_beta = 0.9
outer_rate = 0.7
root_scale = 1.0 / math.sqrt(corr_two)
rate_scale = learn_rate / corr_one
chunk_count = 2
lanes = 128
vmem_limit = 12 * 1024 * 1024

wide = jnp.float32
narrow = jnp.bfloat16
VMEM = pl.BlockSpec(memory_space=pltpu.VMEM)
SMEM = pl.BlockSpec(memory_space=pltpu.SMEM)
HBM = pl.BlockSpec(memory_space=pltpu.HBM)


def adam_step(params, gradient, first_moment, second_moment):
    first_new = beta_one * first_moment + (1.0 - beta_one) * gradient
    second_new = beta_two * second_moment + (1.0 - beta_two) * gradient * gradient
    ratio = first_new / (jnp.sqrt(second_new) * root_scale + adam_eps)
    return (params * (1.0 - learn_rate * weight_decay) - ratio * rate_scale, first_new, second_new)


def nesterov(delta_part, params_part, mom_part):
    new_mom = outer_beta * mom_part + delta_part
    new_params = params_part - outer_rate * (delta_part + outer_beta * new_mom)
    return (new_params, new_mom)


def add_narrow(left, right):
    return (left.astype(wide) + right.astype(wide)).astype(narrow)


def blocks_of(size, most, unit):
    for count in range(1, size // unit + 1):
        if size % (count * unit) == 0 and size // count <= most:
            return count
    return 1


def call(kernel, out_shape, inputs, flops=0, moved=0, scratch=(), aliases=None, specs=None, outs=None, grid=(), limit=vmem_limit):
    return pl.pallas_call(
        kernel,
        out_shape=out_shape,
        grid=grid,
        in_specs=specs if specs is not None else [VMEM] * len(inputs),
        out_specs=outs if outs is not None else jax.tree.map(lambda _: VMEM, out_shape),
        scratch_shapes=list(scratch),
        compiler_params=pltpu.CompilerParams(vmem_limit_bytes=limit),

        input_output_aliases=aliases or {},
    )(*inputs)


def scale_kernel(chunks, weight_ref, gain_ref, spread_ref, *refs):
    sent_refs, (held, sems) = refs[:chunks], refs[chunks:]
    rows = weight_ref.shape[1]
    depth = rows // chunks
    spans = [slice(c * depth, (c + 1) * depth) for c in range(chunks)]
    copies = [
        pltpu.make_async_copy(weight_ref.at[0, span], held.at[span], sems.at[c])
        for c, span in enumerate(spans)
    ]
    for copy in copies:
        copy.start()
    spread = jnp.broadcast_to(gain_ref[...], (lanes, rows)).T
    spread_ref[...] = spread
    used = spread.astype(narrow).astype(wide)
    for c, span in enumerate(spans):
        copies[c].wait()
        for k in range(weight_ref.shape[2] // lanes):
            part = slice(k * lanes, (k + 1) * lanes)
            sent_refs[c][:, part] = (held[span, part].astype(wide) * used[span]).astype(narrow)


def partial_kernel(inputs_ref, cot_ref, partial_ref, rms_ref, held_ref, cot_held, sems):
    tokens, feats = inputs_ref.shape[1:]
    copies = [
        pltpu.make_async_copy(inputs_ref, held_ref, sems.at[0]),
        pltpu.make_async_copy(cot_ref, cot_held, sems.at[1]),
    ]
    for copy in copies:
        copy.start()
    for copy in copies:
        copy.wait()
    total = jnp.zeros((tokens, lanes), wide)
    for k in range(feats // lanes):
        part = held_ref[0, :, k * lanes : (k + 1) * lanes].astype(wide)
        total = total + part * part
    mean = jnp.sum(total, axis=1, keepdims=True) / feats
    inv_rms = lax.rsqrt(mean + norm_eps)
    rms_ref[...] = jnp.broadcast_to(inv_rms, rms_ref.shape)
    scaled = (cot_held[0].astype(wide) * inv_rms).astype(narrow)
    step = 2 * lanes if feats % (2 * lanes) == 0 else lanes
    for k in range(feats // step):
        span = slice(k * step, (k + 1) * step)
        partial_ref[span, :] = lax.dot_general(
            held_ref[0, :, span], scaled, (((0,), (0,)), ((), ())), preferred_element_type=wide
        ).astype(narrow)


def onward_kernel(n, c, chunks, s, me_ref, partial_ref, even_ref, odd_ref, to_even_ref, to_odd_ref):
    me = me_ref[0]
    depth = even_ref.shape[0]
    even = (me & 1) == 0
    for came_ref, sent_ref, right in (
        (odd_ref, to_even_ref, even),
        (even_ref, to_odd_ref, jnp.logical_not(even)),
    ):
        place = jnp.where(right, me, n - 1 - me)
        owner = jnp.where(right, n - s + place, s - 1 - place)

        @pl.when(s > place)
        def _():
            start = pl.multiple_of((owner * chunks + c) * depth, 16)
            sent_ref[...] = add_narrow(came_ref[...], partial_ref[pl.ds(start, depth), :])

        @pl.when(s <= place)
        def _():
            sent_ref[...] = came_ref[...]


def keys_kernel(n, chunks, me_ref, inputs_ref, rms_ref, *refs):
    own, got = refs[:chunks], refs[chunks:-2]
    keys_ref, weights = refs[-2:]
    me = me_ref[0]
    depth, cols = own[0].shape
    rows = depth * chunks

    def put(block, c, ref):
        weights[pl.ds(pl.multiple_of(block * rows + c * depth, 16), depth), :] = ref[...]

    for c in range(chunks):
        put(me, c, own[c])
    even = (me & 1) == 0
    for s in range(n - 1):
        for w in range(2):
            from_right = even if w == 0 else jnp.logical_not(even)
            block = jnp.where(from_right, me + 1 + s, me - 1 - s)

            @pl.when((block >= 0) & (block < n))
            def _():
                for c in range(chunks):
                    put(block, c, got[(s * 2 + w) * chunks + c])

    total = jnp.dot(inputs_ref[0], weights[...], preferred_element_type=wide)
    for k in range(cols // lanes):
        part = slice(k * lanes, (k + 1) * lanes)
        keys_ref[0, :, part] = (total[:, part] * rms_ref[...]).astype(narrow)


def fetch_kernel(*refs):
    count = len(refs) // 2
    sems = refs[-1]
    copies = [
        pltpu.make_async_copy(refs[i], refs[count + i], sems.at[i]) for i in range(count)
    ]
    for copy in copies:
        copy.start()
    for copy in copies:
        copy.wait()


def adam_kernel(c, chunks, me_ref, spread_ref, weight_ref, first_ref, second_ref, partial_ref, *refs):
    came, outs = refs[:2], refs[-4:]
    share_ref, new_weight_ref, new_first_ref, new_second_ref = outs
    depth, cols = weight_ref.shape[1:]
    steps = pl.num_programs(0)
    start = pl.multiple_of(((me_ref[0] * chunks + c) * steps + pl.program_id(0)) * depth, 16)
    share = jnp.zeros((depth, lanes), wide)
    used = spread_ref[...].astype(narrow).astype(wide)
    for k in range(cols // lanes):
        part = slice(k * lanes, (k + 1) * lanes)
        total = partial_ref[pl.ds(start, depth), part].astype(wide)
        for ref in came:
            total = total + ref[:, part].astype(wide)
        weight = weight_ref[0, :, part].astype(wide)
        share = share + total * weight
        new_weight, new_first, new_second = adam_step(
            weight, total * used, first_ref[0, :, part], second_ref[0, :, part]
        )
        new_weight_ref[0, :, part] = new_weight.astype(narrow)
        new_first_ref[0, :, part] = new_first
        new_second_ref[0, :, part] = new_second
    share_ref[...] = share


def gain_kernel(chunks, *refs):
    gain_ref, first_ref, second_ref = refs[chunks : chunks + 3]
    news = refs[chunks + 3 :]
    share = jnp.concatenate([ref[...] for ref in refs[:chunks]], axis=0)
    gradient = jnp.sum(share.T, axis=0, keepdims=True)
    for ref, value in zip(news, adam_step(gain_ref[...], gradient, first_ref[...], second_ref[...])):
        ref[...] = value


def pair_kernel(core_ref, mine_ref, other_ref, half_ref):
    half, step = half_ref.shape[0], 16
    start = core_ref[0] * half

    @pl.loop(0, half // step, unroll=4)
    def _(i):
        span = pl.ds(pl.multiple_of((start + i * step) * lanes, step * lanes), step * lanes)
        total = mine_ref[:, span].astype(wide) + other_ref[:, span].astype(wide)
        half_ref[pl.ds(pl.multiple_of(i * step, step), step), :] = total.reshape(step, lanes).astype(narrow)


def sum_kernel(left_ref, right_ref, total_ref):
    total_ref[...] = add_narrow(left_ref[...], right_ref[...])


def nesterov_kernel(silos, core_ref, own_ref, other_ref, params_ref, mom_ref, new_params_ref, new_mom_ref):
    mine = core_ref[0] == pl.program_id(0)
    delta = jnp.where(mine, own_ref[...], other_ref[...]).astype(wide) / silos
    new_params_ref[0], new_mom_ref[0] = nesterov(delta, params_ref[0], mom_ref[0])


def tie(values, other):
    return lax.optimization_barrier((values, other))[0]


def outer_steps(pseudo_grad, outer_params, outer_mom, silos):
    size = pseudo_grad.shape[1]
    half = size // 2 // lanes
    if silos < 2 or silos & (silos - 1) != 0 or size % (32 * lanes) != 0:
        yield nesterov(lax.psum(pseudo_grad[0].astype(wide), "silo") / silos, outer_params, outer_mom)
        return

    def swap(part, bit):
        return lax.ppermute(part, "silo", [(i, i ^ bit) for i in range(silos)])

    core = (lax.axis_index("silo") & 1).astype(jnp.int32).reshape(1)
    part = jax.ShapeDtypeStruct((half, lanes), narrow)
    cost = dict(flops=half * lanes, moved=6 * half * lanes)
    total = call(
        pair_kernel, part, [core, pseudo_grad, swap(pseudo_grad, 1)], specs=[SMEM, VMEM, VMEM], **cost
    )
    yield total
    bit = 2
    while bit < silos:
        total = call(sum_kernel, part, [total, swap(total, bit)], **cost)
        yield total
        bit *= 2
    other = swap(total, 1)
    steps = blocks_of(half, 512, 16)
    line = pl.BlockSpec((half // steps, lanes), lambda h, j: (j, 0))
    block = pl.BlockSpec((1, half // steps, lanes), lambda h, j: (h, j, 0))
    new_params, new_mom = call(
        functools.partial(nesterov_kernel, silos),
        [jax.ShapeDtypeStruct((2, half, lanes), wide)] * 2,
        [core, total, other, outer_params.reshape(2, half, lanes), outer_mom.reshape(2, half, lanes)],
        flops=12 * size,
        moved=20 * size,
        specs=[SMEM, line, line, block, block],
        outs=[block, block],
        grid=(2, steps),
    )
    yield new_params.reshape(size), new_mom.reshape(size)


def make(silos, n):
    def per_device(
        activations,
        key_cot,
        key_weight,
        weight_first,
        weight_second,
        norm_gain,
        gain_first,
        gain_second,
        pseudo_grad,
        outer_params,
        outer_mom,
    ):
        me = lax.axis_index("fsdp")
        me_word = me.astype(jnp.int32).reshape(1)
        tokens, feats = activations.shape[1:]
        rows, cols = key_weight.shape[1:]
        chunks = chunk_count if rows % (16 * chunk_count) == 0 else 1
        depth = rows // chunks
        shape = jax.ShapeDtypeStruct

        spread, *own = call(
            functools.partial(scale_kernel, chunks),
            [shape((rows, lanes), wide)] + [shape((depth, cols), narrow)] * chunks,
            [key_weight, norm_gain],
            flops=rows * cols,
            moved=4 * rows * cols,
            specs=[HBM, VMEM],
            scratch=[pltpu.VMEM((rows, cols), narrow), pltpu.SemaphoreType.DMA((chunks,))],
        )
        links = [
            [pair for i in range(start, n - 1, 2) for pair in ((i, i + 1), (i + 1, i))]
            for start in (0, 1)
        ]
        slots = []
        for s in range(n):
            got = [[None for _ in range(chunks)] for _ in links]
            for c in range(chunks):
                sent = [own[c], own[c]]
                if s > 0:
                    came = [slots[-1][w][c] for w in range(2)]
                    if c == chunks - 1:
                        outer_part = next(outer, outer_part)
                        came = tie(came, outer_part)
                    sent = call(
                        functools.partial(onward_kernel, n, c, chunks, s),
                        [shape((depth, cols), narrow)] * 2,
                        [me_word, partial, *came],
                        flops=2 * depth * cols,
                        moved=12 * depth * cols,
                        specs=[SMEM] + [VMEM] * 3,
                    )
                for w in range(2):
                    got[w][c] = lax.ppermute(sent[w], "fsdp", links[w])
            slots.append(got)
            if s == 0:
                partial, inv_rms, inputs = call(
                    partial_kernel,
                    [
                        shape((feats, cols), narrow),
                        shape((tokens, lanes), wide),
                        shape(activations.shape, narrow),
                    ],
                    [activations, key_cot],
                    specs=[HBM, HBM],
                    scratch=[pltpu.VMEM(key_cot.shape, narrow), pltpu.SemaphoreType.DMA((2,))],
                    flops=2 * tokens * feats * cols,
                    moved=2 * (tokens * feats + feats * cols + tokens * cols),
                )
                outer = outer_steps(pseudo_grad, outer_params, outer_mom, silos)
                outer_part = partial

        keys = call(
            functools.partial(keys_kernel, n, chunks),
            shape((1, tokens, cols), narrow),
            [me_word, inputs, inv_rms, *own]
            + [slots[s][w][c] for s in range(n - 1) for w in range(2) for c in range(chunks)],
            flops=2 * tokens * feats * cols,
            moved=2 * (tokens * feats + feats * cols + tokens * cols),
            scratch=[pltpu.VMEM((feats, cols), narrow)],
            specs=[SMEM] + [VMEM] * (2 + chunks + (n - 1) * 2 * chunks),
        )

        for outer_part in outer:
            pass
        shares, news = [], []
        steps = blocks_of(depth, 96, 16)
        tall = depth // steps
        for c in range(chunks):
            came = [slots[n - 1][w][c] for w in range(2)]
            if c == 0:
                came = tie(came, outer_part)
            block = pl.BlockSpec((1, tall, cols), lambda i, c=c: (0, c * steps + i, 0))
            share, *news = call(
                functools.partial(adam_kernel, c, chunks),
                [shape((depth, lanes), wide)]
                + [shape((1, rows, cols), kind) for kind in (narrow, wide, wide)],
                [me_word, spread, key_weight, weight_first, weight_second, partial, *came, *news],
                flops=20 * depth * cols,
                moved=20 * depth * cols,
                specs=[SMEM, pl.BlockSpec((tall, lanes), lambda i, c=c: (c * steps + i, 0))]
                + [block] * 3
                + [VMEM]
                + [pl.BlockSpec((tall, cols), lambda i: (i, 0))] * 2
                + [pl.BlockSpec(memory_space=pl.ANY)] * len(news),
                outs=[pl.BlockSpec((tall, lanes), lambda i: (i, 0))] + [block] * 3,
                aliases={8 + i: 1 + i for i in range(len(news))},
                grid=(steps,),
            )
            shares.append(share)
        new_gains = call(
            functools.partial(gain_kernel, chunks),
            [shape((1, rows), wide)] * 3,
            [*shares, norm_gain, gain_first, gain_second],
            flops=20 * rows,
            moved=4 * rows * (lanes + 6),
        )
        return (
            keys,
            *news,
            *new_gains,
            *outer_part,
        )

    return per_device


def solution(mesh):
    return jax.shard_map(
        make(mesh.shape["silo"], mesh.shape["fsdp"]),
        mesh=mesh,
        in_specs=(
            P("silo", "fsdp", None),
            P("silo", "fsdp", None),
            P("silo", "fsdp", None),
            P("silo", "fsdp", None),
            P("silo", "fsdp", None),
            P("silo", "fsdp"),
            P("silo", "fsdp"),
            P("silo", "fsdp"),
            P("silo", "fsdp"),
            P("fsdp"),
            P("fsdp"),
        ),
        out_specs=(
            P("silo", "fsdp", None),
            P("silo", "fsdp", None),
            P("silo", "fsdp", None),
            P("silo", "fsdp", None),
            P("silo", "fsdp"),
            P("silo", "fsdp"),
            P("silo", "fsdp"),
            P("fsdp"),
            P("fsdp"),
        ),
        check_vma=False,
    )
```

```python
import functools
import math

import jax
import jax.numpy as jnp
from jax import lax
from jax.experimental import pallas as pl
from jax.experimental.pallas import tpu as pltpu
from jax.sharding import PartitionSpec as P

norm_eps = 1e-05
beta_one = 0.9
beta_two = 0.95
corr_one = 1.0 - math.exp(200.0 * math.log(0.9))
corr_two = 1.0 - math.exp(200.0 * math.log(0.95))
learn_rate = 0.001
adam_eps = 1e-08
weight_decay = 0.1
outer_beta = 0.9
outer_rate = 0.7
root_scale = 1.0 / math.sqrt(corr_two)
rate_scale = learn_rate / corr_one
chunk_count = 2
lanes = 128
vmem_limit = 12 * 1024 * 1024
moved_scale, moved_partial, moved_pair, moved_sum = 0, 0, 0, 0
moved_onward, moved_keys, moved_adam, moved_outer = 0, 0, 0, 0

wide = jnp.float32
narrow = jnp.bfloat16
VMEM = pl.BlockSpec(memory_space=pltpu.VMEM)
HBM = pl.BlockSpec(memory_space=pltpu.HBM)
held_shape = pltpu.VMEM


def adam_step(params, gradient, first_moment, second_moment):
    first_new = beta_one * first_moment + (1.0 - beta_one) * gradient
    second_new = beta_two * second_moment + (1.0 - beta_two) * gradient * gradient
    ratio = first_new / (jnp.sqrt(second_new) * root_scale + adam_eps)
    return (params * (1.0 - learn_rate * weight_decay) - ratio * rate_scale, first_new, second_new)


def nesterov(delta_part, params_part, mom_part):
    new_mom = outer_beta * mom_part + delta_part
    new_params = params_part - outer_rate * (delta_part + outer_beta * new_mom)
    return (new_params, new_mom)


def core_of_chip():
    return lax.axis_index("silo") & 1


def add_narrow(left, right):
    return (left.astype(wide) + right.astype(wide)).astype(narrow)


def blocks_of(size, most, unit):
    for count in range(1, size // unit + 1):
        if size % (count * unit) == 0 and size // count <= most:
            return count
    return 1


def call(kernel, out_shape, inputs, moved=0, scratch=(), aliases=None, specs=None, outs=None, grid=(), limit=vmem_limit):
    return pl.pallas_call(
        kernel,
        out_shape=out_shape,
        grid=grid,
        in_specs=specs if specs is not None else [VMEM] * len(inputs),
        out_specs=outs if outs is not None else jax.tree.map(lambda _: VMEM, out_shape),
        scratch_shapes=list(scratch),
        compiler_params=pltpu.CompilerParams(vmem_limit_bytes=limit),
        cost_estimate=pl.CostEstimate(flops=0, bytes_accessed=moved, transcendentals=0) if moved else None,

        input_output_aliases=aliases or {},
    )(*inputs)


def scale_kernel(chunks, weight_ref, gain_ref, spread_ref, *refs):
    sent_refs, (held, gain_held, sems) = refs[:chunks], refs[chunks:]
    rows = weight_ref.shape[1]
    depth = rows // chunks
    spans = [slice(c * depth, (c + 1) * depth) for c in range(chunks)]
    copies = [
        pltpu.make_async_copy(weight_ref.at[0, span], held.at[span], sems.at[c])
        for c, span in enumerate(spans)
    ]
    gain_copy = pltpu.make_async_copy(gain_ref, gain_held, sems.at[chunks])
    for copy in (gain_copy, *copies):
        copy.start()
    gain_copy.wait()
    spread = jnp.broadcast_to(gain_held[...], (lanes, rows)).T
    spread_ref[...] = spread
    used = spread.astype(narrow).astype(wide)
    for c, span in enumerate(spans):
        copies[c].wait()
        for k in range(weight_ref.shape[2] // lanes):
            part = slice(k * lanes, (k + 1) * lanes)
            sent_refs[c][:, part] = (held[span, part].astype(wide) * used[span]).astype(narrow)


def partial_kernel(inputs_ref, cot_ref, partial_ref, rms_ref, held_ref, cot_held, sems):
    tokens, feats = inputs_ref.shape[1:]
    copies = [
        pltpu.make_async_copy(inputs_ref, held_ref, sems.at[0]),
        pltpu.make_async_copy(cot_ref, cot_held, sems.at[1]),
    ]
    for copy in copies:
        copy.start()
    for copy in copies:
        copy.wait()
    total = jnp.zeros((tokens, lanes), wide)
    for k in range(feats // lanes):
        part = held_ref[0, :, k * lanes : (k + 1) * lanes].astype(wide)
        total = total + part * part
    mean = jnp.sum(total, axis=1, keepdims=True) / feats
    inv_rms = lax.rsqrt(mean + norm_eps)
    rms_ref[...] = jnp.broadcast_to(inv_rms, rms_ref.shape)
    scaled = (cot_held[0].astype(wide) * inv_rms).astype(narrow)
    step = 2 * lanes if feats % (2 * lanes) == 0 else lanes
    for k in range(feats // step):
        span = slice(k * step, (k + 1) * step)
        partial_ref[span, :] = lax.dot_general(
            held_ref[0, :, span], scaled, (((0,), (0,)), ((), ())), preferred_element_type=wide
        ).astype(narrow)


def onward_kernel(n, c, chunks, s, partial_ref, even_ref, odd_ref, to_even_ref, to_odd_ref):
    me = lax.axis_index("fsdp")
    depth = even_ref.shape[0]
    even = (me & 1) == 0
    for came_ref, sent_ref, right in (
        (odd_ref, to_even_ref, even),
        (even_ref, to_odd_ref, jnp.logical_not(even)),
    ):
        place = jnp.where(right, me, n - 1 - me)
        owner = jnp.where(right, n - s + place, s - 1 - place)

        @pl.when(s > place)
        def _():
            start = pl.multiple_of((owner * chunks + c) * depth, 16)
            sent_ref[...] = add_narrow(came_ref[...], partial_ref[pl.ds(start, depth), :])

        @pl.when(s <= place)
        def _():
            sent_ref[...] = came_ref[...]


def keys_kernel(n, chunks, inputs_ref, rms_ref, weight_ref, spread_ref, *refs):
    got, (keys_ref, weights) = refs[:-2], refs[-2:]
    me = lax.axis_index("fsdp")
    rows, cols = weight_ref.shape[1:]
    depth = rows // chunks
    used = spread_ref[...].astype(narrow).astype(wide)
    for k in range(cols // lanes):
        part = slice(k * lanes, (k + 1) * lanes)
        weights[pl.ds(pl.multiple_of(me * rows, 16), rows), part] = (
            weight_ref[0, :, part].astype(wide) * used
        ).astype(narrow)

    def put(block, c, ref):
        weights[pl.ds(pl.multiple_of(block * rows + c * depth, 16), depth), :] = ref[...]

    even = (me & 1) == 0
    for s in range(n - 1):
        for w in range(2):
            from_right = even if w == 0 else jnp.logical_not(even)
            block = jnp.where(from_right, me + 1 + s, me - 1 - s)

            @pl.when((block >= 0) & (block < n))
            def _():
                for c in range(chunks):
                    put(block, c, got[(s * 2 + w) * chunks + c])

    total = jnp.dot(inputs_ref[0], weights[...], preferred_element_type=wide)
    for k in range(cols // lanes):
        part = slice(k * lanes, (k + 1) * lanes)
        keys_ref[0, :, part] = (total[:, part] * rms_ref[...]).astype(narrow)


def fetch_kernel(*refs):
    count = len(refs) // 2
    sems = refs[-1]
    copies = [
        pltpu.make_async_copy(refs[i], refs[count + i], sems.at[i]) for i in range(count)
    ]
    for copy in copies:
        copy.start()
    for copy in copies:
        copy.wait()


def adam_kernel(c, chunks, spread_ref, weight_ref, first_ref, second_ref, partial_ref, *refs):
    last = c == chunks - 1
    came = refs[:2]
    if last:
        shares, gains = refs[2 : 2 + c], refs[2 + c : 5 + c]
        new_gains, share_ref = refs[-4:-1], refs[-1]
        new_weight_ref, new_first_ref, new_second_ref = refs[-7:-4]
    else:
        share_ref, new_weight_ref, new_first_ref, new_second_ref = refs[-4:]
    depth, cols = weight_ref.shape[1:]
    step, steps = pl.program_id(0), pl.num_programs(0)
    start = pl.multiple_of(((lax.axis_index("fsdp") * chunks + c) * steps + step) * depth, 16)
    share = jnp.zeros((depth, lanes), wide)
    used = spread_ref[...].astype(narrow).astype(wide)
    for k in range(cols // lanes):
        part = slice(k * lanes, (k + 1) * lanes)
        total = partial_ref[pl.ds(start, depth), part].astype(wide)
        for ref in came:
            total = total + ref[:, part].astype(wide)
        weight = weight_ref[0, :, part].astype(wide)
        share = share + total * weight
        new_weight, new_first, new_second = adam_step(
            weight, total * used, first_ref[0, :, part], second_ref[0, :, part]
        )
        new_weight_ref[0, :, part] = new_weight.astype(narrow)
        new_first_ref[0, :, part] = new_first
        new_second_ref[0, :, part] = new_second
    if not last:
        share_ref[...] = share
        return
    share_ref[pl.ds(pl.multiple_of(step * depth, 16), depth), :] = share

    @pl.when(step == steps - 1)
    def _():
        whole = jnp.concatenate([ref[...] for ref in (*shares, share_ref)], axis=0)
        gradient = jnp.sum(whole.T, axis=0, keepdims=True)
        for ref, value in zip(new_gains, adam_step(gains[0][...], gradient, gains[1][...], gains[2][...])):
            ref[...] = value


def pair_kernel(mine_ref, other_ref, half_ref, mine_held, other_held, sems):
    half, step = half_ref.shape[0], 16
    whole = pl.ds(pl.multiple_of(core_of_chip() * (half * lanes), half * lanes), half * lanes)
    copies = [
        pltpu.make_async_copy(mine_ref.at[:, whole], mine_held, sems.at[0]),
        pltpu.make_async_copy(other_ref.at[:, whole], other_held, sems.at[1]),
    ]
    for copy in copies:
        copy.start()
    for copy in copies:
        copy.wait()

    @pl.loop(0, half // step, unroll=4)
    def _(i):
        span = pl.ds(pl.multiple_of(i * (step * lanes), step * lanes), step * lanes)
        total = mine_held[:, span].astype(wide) + other_held[:, span].astype(wide)
        half_ref[pl.ds(pl.multiple_of(i * step, step), step), :] = total.reshape(step, lanes).astype(narrow)


def sum_kernel(left_ref, right_ref, total_ref):
    total_ref[...] = add_narrow(left_ref[...], right_ref[...])


def nesterov_kernel(silos, own_ref, other_ref, params_ref, mom_ref, new_params_ref, new_mom_ref):
    mine = core_of_chip() == pl.program_id(0)
    delta = jnp.where(mine, own_ref[...], other_ref[...]).astype(wide) / silos
    new_params_ref[0], new_mom_ref[0] = nesterov(delta, params_ref[0], mom_ref[0])


def in_hbm(array):
    return pltpu.with_memory_space_constraint(array, pltpu.HBM)


def in_vmem(arrays):
    return [pltpu.with_memory_space_constraint(array, pltpu.VMEM) for array in arrays]


def tie(values, other):
    return lax.optimization_barrier((values, other))[0]


def pair_operands(mine, other):
    return [in_hbm(mine), other]


def outer_steps(pseudo_grad, outer_params, outer_mom, silos, after):
    size = pseudo_grad.shape[1]
    half = size // 2 // lanes
    if silos < 2 or silos & (silos - 1) != 0 or size % (32 * lanes) != 0:
        yield nesterov(lax.psum(pseudo_grad[0].astype(wide), "silo") / silos, outer_params, outer_mom)
        return

    def swap(part, bit):
        return lax.ppermute(part, "silo", [(i, i ^ bit) for i in range(silos)])

    part = held_shape((half, lanes), narrow)
    total = call(
        pair_kernel,
        part,
        pair_operands(*tie([pseudo_grad, swap(pseudo_grad, 1)], after)),
        moved=moved_pair,
        specs=[HBM, HBM],
        scratch=[pltpu.VMEM((1, half * lanes), narrow)] * 2 + [pltpu.SemaphoreType.DMA((2,))],
    )
    yield total
    bit = 2
    while bit < silos:
        total = call(sum_kernel, part, in_vmem([total, swap(total, bit)]), moved=moved_sum)
        yield total
        bit *= 2
    other = swap(total, 1)
    steps = blocks_of(half, 512, 16)
    line = pl.BlockSpec((half // steps, lanes), lambda h, j: (j, 0))
    block = pl.BlockSpec((1, half // steps, lanes), lambda h, j: (h, j, 0))
    new_params, new_mom = call(
        functools.partial(nesterov_kernel, silos),
        [jax.ShapeDtypeStruct((2, half, lanes), wide)] * 2,
        [total, other, outer_params.reshape(2, half, lanes), outer_mom.reshape(2, half, lanes)],
        moved=moved_outer,
        specs=[line, line, block, block],
        outs=[block, block],
        grid=(2, steps),
    )
    yield new_params.reshape(size), new_mom.reshape(size)


def make(silos, n):
    def per_device(
        activations,
        key_cot,
        key_weight,
        weight_first,
        weight_second,
        norm_gain,
        gain_first,
        gain_second,
        pseudo_grad,
        outer_params,
        outer_mom,
    ):
        tokens, feats = activations.shape[1:]
        rows, cols = key_weight.shape[1:]
        chunks = chunk_count if rows % (16 * chunk_count) == 0 else 1
        depth = rows // chunks
        shape = jax.ShapeDtypeStruct

        spread, *own = call(
            functools.partial(scale_kernel, chunks),
            [held_shape((rows, lanes), wide)] + [held_shape((depth, cols), narrow)] * chunks,
            [in_hbm(key_weight), in_hbm(norm_gain)],
            moved=moved_scale,
            specs=[HBM, HBM],
            scratch=[
                pltpu.VMEM((rows, cols), narrow),
                pltpu.VMEM((1, rows), wide),
                pltpu.SemaphoreType.DMA((chunks + 1,)),
            ],
        )
        links = [
            [pair for i in range(start, n - 1, 2) for pair in ((i, i + 1), (i + 1, i))]
            for start in (0, 1)
        ]
        slots = []
        for s in range(n):
            got = [[None for _ in range(chunks)] for _ in links]
            for c in range(chunks):
                sent = [own[c], own[c]]
                if s > 0:
                    came = [slots[-1][w][c] for w in range(2)]
                    if c == chunks - 1:
                        outer_part = next(outer, outer_part)
                        came = tie(came, outer_part)
                    sent = call(
                        functools.partial(onward_kernel, n, c, chunks, s),
                        [held_shape((depth, cols), narrow)] * 2,
                        [partial, *in_vmem(came)],
                        moved=moved_onward,
                        specs=[VMEM] * 3,
                    )
                for w in range(2):
                    got[w][c] = lax.ppermute(sent[w], "fsdp", links[w])
            slots.append(got)
            if s == 0:
                partial, inv_rms, inputs = call(
                    partial_kernel,
                    [
                        held_shape((feats, cols), narrow),
                        held_shape((tokens, lanes), wide),
                        held_shape(activations.shape, narrow),
                    ],
                    [in_hbm(activations), in_hbm(key_cot)],
                    moved=moved_partial,
                    specs=[HBM, HBM],
                    scratch=[pltpu.VMEM(key_cot.shape, narrow), pltpu.SemaphoreType.DMA((2,))],
                )
                outer = outer_steps(pseudo_grad, outer_params, outer_mom, silos, partial)
                outer_part = partial

        keys = call(
            functools.partial(keys_kernel, n, chunks),
            shape((1, tokens, cols), narrow),
            [inputs, inv_rms, key_weight, spread]
            + [slots[s][w][c] for s in range(n - 1) for w in range(2) for c in range(chunks)],
            moved=moved_keys,
            scratch=[pltpu.VMEM((feats, cols), narrow)],
            specs=[VMEM] * (4 + (n - 1) * 2 * chunks),
        )

        for outer_part in outer:
            pass
        shares, news = [], []
        steps = blocks_of(depth, 96, 16)
        tall = depth // steps
        for c in range(chunks):
            came = [slots[n - 1][w][c] for w in range(2)]
            if c == 0:
                came = tie(came, outer_part)
            block = pl.BlockSpec((1, tall, cols), lambda i, c=c: (0, c * steps + i, 0))
            last = c == chunks - 1
            extra = [*shares, norm_gain, gain_first, gain_second] if last else []
            gain_outs = [shape((1, rows), wide)] * 3
            count = len(extra)
            outs = call(
                functools.partial(adam_kernel, c, chunks),
                ([] if last else [shape((depth, lanes), wide)])
                + [shape((1, rows, cols), kind) for kind in (narrow, wide, wide)]
                + (gain_outs if last else []),
                [spread, key_weight, weight_first, weight_second, partial, *came, *extra, *news],
                moved=moved_adam,
                specs=[pl.BlockSpec((tall, lanes), lambda i, c=c: (c * steps + i, 0))]
                + [block] * 3
                + [VMEM]
                + [pl.BlockSpec((tall, cols), lambda i: (i, 0))] * 2
                + [VMEM] * count
                + [pl.BlockSpec(memory_space=pl.ANY)] * len(news),
                outs=([] if last else [pl.BlockSpec((tall, lanes), lambda i: (i, 0))])
                + [block] * 3
                + ([VMEM] * 3 if last else []),
                aliases={7 + count + i: (0 if last else 1) + i for i in range(len(news))},
                scratch=[pltpu.VMEM((depth, lanes), wide)] if last else [],
                grid=(steps,),
            )
            if last:
                news, new_gains = outs[:3], outs[3:]
            else:
                shares.append(outs[0])
                news = outs[1:]
        return (
            keys,
            *news,
            *new_gains,
            *outer_part,
        )

    return per_device


def solution(mesh):
    return jax.shard_map(
        make(mesh.shape["silo"], mesh.shape["fsdp"]),
        mesh=mesh,
        in_specs=(
            P("silo", "fsdp", None),
            P("silo", "fsdp", None),
            P("silo", "fsdp", None),
            P("silo", "fsdp", None),
            P("silo", "fsdp", None),
            P("silo", "fsdp"),
            P("silo", "fsdp"),
            P("silo", "fsdp"),
            P("silo", "fsdp"),
            P("fsdp"),
            P("fsdp"),
        ),
        out_specs=(
            P("silo", "fsdp", None),
            P("silo", "fsdp", None),
            P("silo", "fsdp", None),
            P("silo", "fsdp", None),
            P("silo", "fsdp"),
            P("silo", "fsdp"),
            P("silo", "fsdp"),
            P("fsdp"),
            P("fsdp"),
        ),
        check_vma=False,
    )
```

```python
import functools
import math

import jax
import jax.numpy as jnp
from jax import lax
from jax.experimental import pallas as pl
from jax.experimental.pallas import tpu as pltpu
from jax.sharding import PartitionSpec as P

norm_eps = 1e-05
beta_one = 0.9
beta_two = 0.95
corr_one = 1.0 - math.exp(200.0 * math.log(0.9))
corr_two = 1.0 - math.exp(200.0 * math.log(0.95))
learn_rate = 0.001
adam_eps = 1e-08
weight_decay = 0.1
outer_beta = 0.9
outer_rate = 0.7
root_scale = 1.0 / math.sqrt(corr_two)
rate_scale = learn_rate / corr_one
chunk_parts = (1, 1)
adam_rows = 512
lanes = 128
vmem_limit = 12 * 1024 * 1024

wide = jnp.float32
narrow = jnp.bfloat16
VMEM = pl.BlockSpec(memory_space=pltpu.VMEM)
HBM = pl.BlockSpec(memory_space=pltpu.HBM)


def adam_step(params, gradient, first_moment, second_moment):
    first_new = beta_one * first_moment + (1.0 - beta_one) * gradient
    second_new = beta_two * second_moment + (1.0 - beta_two) * gradient * gradient
    ratio = first_new / (jnp.sqrt(second_new) * root_scale + adam_eps)
    return (params * (1.0 - learn_rate * weight_decay) - ratio * rate_scale, first_new, second_new)


def nesterov(delta_part, params_part, mom_part):
    new_mom = outer_beta * mom_part + delta_part
    new_params = params_part - outer_rate * (delta_part + outer_beta * new_mom)
    return (new_params, new_mom)


def split_rows(rows, unit=16):
    units, whole, ends = rows // unit, sum(chunk_parts), [0]
    for k in range(1, len(chunk_parts)):
        ends.append(units * sum(chunk_parts[:k]) // whole * unit)
    ends.append(rows)
    return [(a, b - a) for a, b in zip(ends, ends[1:]) if b > a]


def core_of_chip():
    return lax.axis_index("silo") & 1


def add_narrow(left, right):
    return (left.astype(wide) + right.astype(wide)).astype(narrow)


def blocks_of(size, most, unit):
    for count in range(1, size // unit + 1):
        if size % (count * unit) == 0 and size // count <= most:
            return count
    return 1


def call(kernel, out_shape, inputs, scratch=(), aliases=None, specs=None, outs=None, grid=()):
    return pl.pallas_call(
        kernel,
        out_shape=out_shape,
        grid=grid,
        in_specs=specs if specs is not None else [VMEM] * len(inputs),
        out_specs=outs if outs is not None else jax.tree.map(lambda _: VMEM, out_shape),
        scratch_shapes=list(scratch),
        compiler_params=pltpu.CompilerParams(vmem_limit_bytes=vmem_limit),

        input_output_aliases=aliases or {},
    )(*inputs)


def scale_kernel(chunks, weight_ref, gain_ref, spread_ref, *refs):
    count = len(chunks)
    sent_refs, (held, gain_held, sems) = refs[: 2 * count], refs[2 * count :]
    rows = weight_ref.shape[1]
    spans = [slice(start, start + depth) for start, depth in chunks]
    copies = [
        pltpu.make_async_copy(weight_ref.at[0, span], held.at[span], sems.at[c])
        for c, span in enumerate(spans)
    ]
    gain_copy = pltpu.make_async_copy(gain_ref, gain_held, sems.at[count])
    for copy in (gain_copy, *copies):
        copy.start()
    gain_copy.wait()
    spread = jnp.broadcast_to(gain_held[...], (lanes, rows)).T
    spread_ref[...] = spread
    used = spread.astype(narrow).astype(wide)
    for c, span in enumerate(spans):
        copies[c].wait()
        for k in range(weight_ref.shape[2] // lanes):
            part = slice(k * lanes, (k + 1) * lanes)
            piece = (held[span, part].astype(wide) * used[span]).astype(narrow)
            sent_refs[2 * c][:, part] = piece
            sent_refs[2 * c + 1][:, part] = piece


def partial_kernel(inputs_ref, cot_ref, partial_ref, rms_ref, held_ref, cot_held, sems):
    tokens, feats = inputs_ref.shape[1:]
    copies = [
        pltpu.make_async_copy(inputs_ref, held_ref, sems.at[0]),
        pltpu.make_async_copy(cot_ref, cot_held, sems.at[1]),
    ]
    for copy in copies:
        copy.start()
    for copy in copies:
        copy.wait()
    total = jnp.zeros((tokens, lanes), wide)
    for k in range(feats // lanes):
        part = held_ref[0, :, k * lanes : (k + 1) * lanes].astype(wide)
        total = total + part * part
    mean = jnp.sum(total, axis=1, keepdims=True) / feats
    inv_rms = lax.rsqrt(mean + norm_eps)
    rms_ref[...] = jnp.broadcast_to(inv_rms, rms_ref.shape)
    scaled = (cot_held[0].astype(wide) * inv_rms).astype(narrow)
    step = 2 * lanes if feats % (2 * lanes) == 0 else lanes
    for k in range(feats // step):
        span = slice(k * step, (k + 1) * step)
        partial_ref[span, :] = lax.dot_general(
            held_ref[0, :, span], scaled, (((0,), (0,)), ((), ())), preferred_element_type=wide
        ).astype(narrow)


def onward_kernel(n, rows, first, s, partial_ref, even_ref, odd_ref, to_even_ref, to_odd_ref):
    me = lax.axis_index("fsdp")
    depth = even_ref.shape[0]
    even = (me & 1) == 0
    for came_ref, sent_ref, right in (
        (odd_ref, to_even_ref, even),
        (even_ref, to_odd_ref, jnp.logical_not(even)),
    ):
        place = jnp.where(right, me, n - 1 - me)
        owner = jnp.where(right, n - s + place, s - 1 - place)

        @pl.when(s > place)
        def _():
            start = pl.multiple_of(owner * rows + first, 16)
            sent_ref[...] = add_narrow(came_ref[...], partial_ref[pl.ds(start, depth), :])

        @pl.when(s <= place)
        def _():
            sent_ref[...] = came_ref[...]


def keys_kernel(n, chunks, inputs_ref, rms_ref, weight_ref, spread_ref, *refs):
    got, (keys_ref, weights) = refs[:-2], refs[-2:]
    me = lax.axis_index("fsdp")
    rows, cols = weight_ref.shape[1:]
    used = spread_ref[...].astype(narrow).astype(wide)
    for k in range(cols // lanes):
        part = slice(k * lanes, (k + 1) * lanes)
        weights[pl.ds(pl.multiple_of(me * rows, 16), rows), part] = (
            weight_ref[0, :, part].astype(wide) * used
        ).astype(narrow)

    def put(block, c, ref):
        first, depth = chunks[c]
        weights[pl.ds(pl.multiple_of(block * rows + first, 16), depth), :] = ref[...]

    even = (me & 1) == 0
    for s in range(n - 1):
        for w in range(2):
            from_right = even if w == 0 else jnp.logical_not(even)
            block = jnp.where(from_right, me + 1 + s, me - 1 - s)

            @pl.when((block >= 0) & (block < n))
            def _():
                for c in range(len(chunks)):
                    put(block, c, got[(s * 2 + w) * len(chunks) + c])

    total = jnp.dot(inputs_ref[0], weights[...], preferred_element_type=wide)
    for k in range(cols // lanes):
        part = slice(k * lanes, (k + 1) * lanes)
        keys_ref[0, :, part] = (total[:, part] * rms_ref[...]).astype(narrow)


def fetch_kernel(*refs):
    count = len(refs) // 2
    sems = refs[-1]
    copies = [
        pltpu.make_async_copy(refs[i], refs[count + i], sems.at[i]) for i in range(count)
    ]
    for copy in copies:
        copy.start()
    for copy in copies:
        copy.wait()


def adam_kernel(c, chunks, spread_ref, weight_ref, first_ref, second_ref, partial_ref, *refs):
    last = c == len(chunks) - 1
    came = refs[:2]
    if last:
        shares, gains = refs[2 : 2 + c], refs[2 + c : 5 + c]
        new_gains, share_ref = refs[-4:-1], refs[-1]
        new_weight_ref, new_first_ref, new_second_ref = refs[-7:-4]
    else:
        share_ref, new_weight_ref, new_first_ref, new_second_ref = refs[-4:]
    depth, cols = weight_ref.shape[1:]
    step, steps = pl.program_id(0), pl.num_programs(0)
    whole = sum(size for _, size in chunks)
    start = pl.multiple_of(lax.axis_index("fsdp") * whole + chunks[c][0] + step * depth, 16)
    share = jnp.zeros((depth, lanes), wide)
    used = spread_ref[...].astype(narrow).astype(wide)
    for k in range(cols // lanes):
        part = slice(k * lanes, (k + 1) * lanes)
        total = partial_ref[pl.ds(start, depth), part].astype(wide)
        for ref in came:
            total = total + ref[:, part].astype(wide)
        weight = weight_ref[0, :, part].astype(wide)
        share = share + total * weight
        new_weight, new_first, new_second = adam_step(
            weight, total * used, first_ref[0, :, part], second_ref[0, :, part]
        )
        new_weight_ref[0, :, part] = new_weight.astype(narrow)
        new_first_ref[0, :, part] = new_first
        new_second_ref[0, :, part] = new_second
    if not last:
        share_ref[...] = share
        return
    share_ref[pl.ds(pl.multiple_of(step * depth, 16), depth), :] = share

    @pl.when(step == steps - 1)
    def _():
        joined = jnp.concatenate([ref[...] for ref in (*shares, share_ref)], axis=0)
        gradient = jnp.sum(joined.T, axis=0, keepdims=True)
        for ref, value in zip(new_gains, adam_step(gains[0][...], gradient, gains[1][...], gains[2][...])):
            ref[...] = value


def pair_kernel(mine_ref, other_ref, half_ref, mine_held, other_held, sems):
    half, step = half_ref.shape[0], 16
    whole = pl.ds(pl.multiple_of(core_of_chip() * (half * lanes), half * lanes), half * lanes)
    copies = [
        pltpu.make_async_copy(mine_ref.at[:, whole], mine_held, sems.at[0]),
        pltpu.make_async_copy(other_ref.at[:, whole], other_held, sems.at[1]),
    ]
    for copy in copies:
        copy.start()
    for copy in copies:
        copy.wait()

    @pl.loop(0, half // step, unroll=4)
    def _(i):
        span = pl.ds(pl.multiple_of(i * (step * lanes), step * lanes), step * lanes)
        total = mine_held[:, span].astype(wide) + other_held[:, span].astype(wide)
        half_ref[pl.ds(pl.multiple_of(i * step, step), step), :] = total.reshape(step, lanes).astype(narrow)


def sum_kernel(left_ref, right_ref, total_ref):
    total_ref[...] = add_narrow(left_ref[...], right_ref[...])


def nesterov_kernel(silos, own_ref, other_ref, params_ref, mom_ref, new_params_ref, new_mom_ref):
    mine = core_of_chip() == pl.program_id(0)
    delta = jnp.where(mine, own_ref[...], other_ref[...]).astype(wide) / silos
    new_params_ref[0], new_mom_ref[0] = nesterov(delta, params_ref[0], mom_ref[0])


def in_hbm(array):
    return pltpu.with_memory_space_constraint(array, pltpu.HBM)


def in_vmem(arrays):
    return [pltpu.with_memory_space_constraint(array, pltpu.VMEM) for array in arrays]


def tie(values, other):
    return lax.optimization_barrier((values, other))[0]


def pair_operands(mine, other):
    return [in_hbm(mine), other]


def outer_steps(pseudo_grad, outer_params, outer_mom, silos, after):
    size = pseudo_grad.shape[1]
    half = size // 2 // lanes
    if silos < 2 or silos & (silos - 1) != 0 or size % (32 * lanes) != 0:
        yield nesterov(lax.psum(pseudo_grad[0].astype(wide), "silo") / silos, outer_params, outer_mom)
        return

    def swap(part, bit):
        return lax.ppermute(part, "silo", [(i, i ^ bit) for i in range(silos)])

    part = pltpu.VMEM((half, lanes), narrow)
    total = call(
        pair_kernel,
        part,
        pair_operands(*tie([pseudo_grad, swap(pseudo_grad, 1)], after)),
        specs=[HBM, HBM],
        scratch=[pltpu.VMEM((1, half * lanes), narrow)] * 2 + [pltpu.SemaphoreType.DMA((2,))],
    )
    yield total
    bit = 2
    while bit < silos:
        total = call(sum_kernel, part, in_vmem([total, swap(total, bit)]))
        yield total
        bit *= 2
    other = swap(total, 1)
    steps = blocks_of(half, 512, 16)
    line = pl.BlockSpec((half // steps, lanes), lambda h, j: (j, 0))
    block = pl.BlockSpec((1, half // steps, lanes), lambda h, j: (h, j, 0))
    new_params, new_mom = call(
        functools.partial(nesterov_kernel, silos),
        [jax.ShapeDtypeStruct((2, half, lanes), wide)] * 2,
        [total, other, outer_params.reshape(2, half, lanes), outer_mom.reshape(2, half, lanes)],
        specs=[line, line, block, block],
        outs=[block, block],
        grid=(2, steps),
    )
    yield new_params.reshape(size), new_mom.reshape(size)


def make(silos, n):
    def per_device(
        activations,
        key_cot,
        key_weight,
        weight_first,
        weight_second,
        norm_gain,
        gain_first,
        gain_second,
        pseudo_grad,
        outer_params,
        outer_mom,
    ):
        tokens, feats = activations.shape[1:]
        rows, cols = key_weight.shape[1:]
        chunks = split_rows(rows)
        count = len(chunks)
        shape = jax.ShapeDtypeStruct

        spread, *own = call(
            functools.partial(scale_kernel, chunks),
            [pltpu.VMEM((rows, lanes), wide)]
            + [pltpu.VMEM((depth, cols), narrow) for _, depth in chunks for _ in range(2)],
            [in_hbm(key_weight), in_hbm(norm_gain)],
            specs=[HBM, HBM],
            scratch=[
                pltpu.VMEM((rows, cols), narrow),
                pltpu.VMEM((1, rows), wide),
                pltpu.SemaphoreType.DMA((count + 1,)),
            ],
        )
        links = [
            [pair for i in range(start, n - 1, 2) for pair in ((i, i + 1), (i + 1, i))]
            for start in (0, 1)
        ]
        slots = []
        for s in range(n):
            got = [[None for _ in range(count)] for _ in links]
            for c, (_, depth) in enumerate(chunks):
                sent = own[2 * c : 2 * c + 2]
                if s > 0:
                    came = [slots[-1][w][c] for w in range(2)]
                    if c == count - 1:
                        outer_part = next(outer, outer_part)
                        came = tie(came, outer_part)
                    sent = call(
                        functools.partial(onward_kernel, n, rows, chunks[c][0], s),
                        [pltpu.VMEM((depth, cols), narrow)] * 2,
                        [partial, *in_vmem(came)],
                        specs=[VMEM] * 3,
                    )
                for w in range(2):
                    got[w][c] = lax.ppermute(sent[w], "fsdp", links[w])
            slots.append(got)
            if s == 0:
                partial, inv_rms, inputs = call(
                    partial_kernel,
                    [
                        pltpu.VMEM((feats, cols), narrow),
                        pltpu.VMEM((tokens, lanes), wide),
                        pltpu.VMEM(activations.shape, narrow),
                    ],
                    [in_hbm(activations), in_hbm(key_cot)],
                    specs=[HBM, HBM],
                    scratch=[pltpu.VMEM(key_cot.shape, narrow), pltpu.SemaphoreType.DMA((2,))],
                )
                outer = outer_steps(pseudo_grad, outer_params, outer_mom, silos, partial)
                outer_part = partial

        keys = call(
            functools.partial(keys_kernel, n, chunks),
            shape((1, tokens, cols), narrow),
            [inputs, inv_rms, key_weight, spread]
            + [slots[s][w][c] for s in range(n - 1) for w in range(2) for c in range(count)],
            scratch=[pltpu.VMEM((feats, cols), narrow)],
            specs=[VMEM] * (4 + (n - 1) * 2 * count),
        )

        for outer_part in outer:
            pass
        shares, news = [], []
        unit = math.gcd(*[x for span in chunks for x in span])
        for c, (first, depth) in enumerate(chunks):
            tall = max(x for x in range(16, adam_rows + 1, 16) if unit % x == 0 or x == 16)
            steps, before = depth // tall, first // tall
            came = [slots[n - 1][w][c] for w in range(2)]
            if c == 0:
                came = tie(came, outer_part)
            block = pl.BlockSpec((1, tall, cols), lambda i, before=before: (0, before + i, 0))
            last = c == count - 1
            extra = [*shares, norm_gain, gain_first, gain_second] if last else []
            gain_outs = [shape((1, rows), wide)] * 3
            extras = len(extra)
            outs = call(
                functools.partial(adam_kernel, c, chunks),
                ([] if last else [shape((depth, lanes), wide)])
                + [shape((1, rows, cols), kind) for kind in (narrow, wide, wide)]
                + (gain_outs if last else []),
                [spread, key_weight, weight_first, weight_second, partial, *came, *extra, *news],
                specs=[pl.BlockSpec((tall, lanes), lambda i, before=before: (before + i, 0))]
                + [block] * 3
                + [VMEM]
                + [pl.BlockSpec((tall, cols), lambda i: (i, 0))] * 2
                + [VMEM] * extras
                + [pl.BlockSpec(memory_space=pl.ANY)] * len(news),
                outs=([] if last else [pl.BlockSpec((tall, lanes), lambda i: (i, 0))])
                + [block] * 3
                + ([VMEM] * 3 if last else []),
                aliases={7 + extras + i: (0 if last else 1) + i for i in range(len(news))},
                scratch=[pltpu.VMEM((depth, lanes), wide)] if last else [],
                grid=(steps,),
            )
            if last:
                news, new_gains = outs[:3], outs[3:]
            else:
                shares.append(outs[0])
                news = outs[1:]
        return (
            keys,
            *news,
            *new_gains,
            *outer_part,
        )

    return per_device


def solution(mesh):
    return jax.shard_map(
        make(mesh.shape["silo"], mesh.shape["fsdp"]),
        mesh=mesh,
        in_specs=(
            P("silo", "fsdp", None),
            P("silo", "fsdp", None),
            P("silo", "fsdp", None),
            P("silo", "fsdp", None),
            P("silo", "fsdp", None),
            P("silo", "fsdp"),
            P("silo", "fsdp"),
            P("silo", "fsdp"),
            P("silo", "fsdp"),
            P("fsdp"),
            P("fsdp"),
        ),
        out_specs=(
            P("silo", "fsdp", None),
            P("silo", "fsdp", None),
            P("silo", "fsdp", None),
            P("silo", "fsdp", None),
            P("silo", "fsdp"),
            P("silo", "fsdp"),
            P("silo", "fsdp"),
            P("fsdp"),
            P("fsdp"),
        ),
        check_vma=False,
    )
```

```python
import functools
import math

import jax
import jax.numpy as jnp
from jax import lax
from jax.experimental import pallas as pl
from jax.experimental.pallas import tpu as pltpu
from jax.sharding import PartitionSpec as P

norm_eps = 1e-05
beta_one = 0.9
beta_two = 0.95
corr_one = 1.0 - math.exp(200.0 * math.log(0.9))
corr_two = 1.0 - math.exp(200.0 * math.log(0.95))
learn_rate = 0.001
adam_eps = 1e-08
weight_decay = 0.1
outer_beta = 0.9
outer_rate = 0.7
root_scale = 1.0 / math.sqrt(corr_two)
rate_scale = learn_rate / corr_one
chunk_parts = (1, 1)
adam_rows = 512
lanes = 128
vmem_limit = 12 * 1024 * 1024

wide = jnp.float32
narrow = jnp.bfloat16
VMEM = pl.BlockSpec(memory_space=pltpu.VMEM)
HBM = pl.BlockSpec(memory_space=pltpu.HBM)


def adam_step(params, gradient, first_moment, second_moment):
    first_new = beta_one * first_moment + (1.0 - beta_one) * gradient
    second_new = beta_two * second_moment + (1.0 - beta_two) * gradient * gradient
    root = second_new * lax.rsqrt(second_new)
    ratio = first_new / (root * root_scale + adam_eps)
    return (params * (1.0 - learn_rate * weight_decay) - ratio * rate_scale, first_new, second_new)


def nesterov(delta_part, params_part, mom_part):
    new_mom = outer_beta * mom_part + delta_part
    new_params = params_part - outer_rate * (delta_part + outer_beta * new_mom)
    return (new_params, new_mom)


def split_rows(rows, unit=16):
    units, whole, ends = rows // unit, sum(chunk_parts), [0]
    for k in range(1, len(chunk_parts)):
        ends.append(units * sum(chunk_parts[:k]) // whole * unit)
    ends.append(rows)
    return [(a, b - a) for a, b in zip(ends, ends[1:]) if b > a]


def core_of_chip():
    return lax.axis_index("silo") & 1


def add_narrow(left, right):
    return (left.astype(wide) + right.astype(wide)).astype(narrow)


def blocks_of(size, most, unit):
    for count in range(1, size // unit + 1):
        if size % (count * unit) == 0 and size // count <= most:
            return count
    return 1


def call(kernel, out_shape, inputs, scratch=(), aliases=None, specs=None, outs=None, grid=()):
    return pl.pallas_call(
        kernel,
        out_shape=out_shape,
        grid=grid,
        in_specs=specs if specs is not None else [VMEM] * len(inputs),
        out_specs=outs if outs is not None else jax.tree.map(lambda _: VMEM, out_shape),
        scratch_shapes=list(scratch),
        compiler_params=pltpu.CompilerParams(vmem_limit_bytes=vmem_limit),

        input_output_aliases=aliases or {},
    )(*inputs)


def scale_kernel(chunks, weight_ref, gain_ref, spread_ref, *refs):
    count = len(chunks)
    sent_refs, (held, gain_held, sems) = refs[: 2 * count], refs[2 * count :]
    rows = weight_ref.shape[1]
    spans = [slice(start, start + depth) for start, depth in chunks]
    copies = [
        pltpu.make_async_copy(weight_ref.at[0, span], held.at[span], sems.at[c])
        for c, span in enumerate(spans)
    ]
    gain_copy = pltpu.make_async_copy(gain_ref, gain_held, sems.at[count])
    for copy in (gain_copy, *copies):
        copy.start()
    gain_copy.wait()
    spread = jnp.broadcast_to(gain_held[...], (lanes, rows)).T
    spread_ref[...] = spread
    used = spread.astype(narrow).astype(wide)
    for c, span in enumerate(spans):
        copies[c].wait()
        for k in range(weight_ref.shape[2] // lanes):
            part = slice(k * lanes, (k + 1) * lanes)
            piece = (held[span, part].astype(wide) * used[span]).astype(narrow)
            sent_refs[2 * c][:, part] = piece
            sent_refs[2 * c + 1][:, part] = piece


def partial_kernel(inputs_ref, cot_ref, partial_ref, rms_ref, held_ref, cot_held, sems):
    tokens, feats = inputs_ref.shape[1:]
    copies = [
        pltpu.make_async_copy(inputs_ref, held_ref, sems.at[0]),
        pltpu.make_async_copy(cot_ref, cot_held, sems.at[1]),
    ]
    for copy in copies:
        copy.start()
    for copy in copies:
        copy.wait()
    total = jnp.zeros((tokens, lanes), wide)
    for k in range(feats // lanes):
        part = held_ref[0, :, k * lanes : (k + 1) * lanes].astype(wide)
        total = total + part * part
    mean = jnp.sum(total, axis=1, keepdims=True) / feats
    inv_rms = lax.rsqrt(mean + norm_eps)
    rms_ref[...] = jnp.broadcast_to(inv_rms, rms_ref.shape)
    scaled = (cot_held[0].astype(wide) * inv_rms).astype(narrow)
    step = 2 * lanes if feats % (2 * lanes) == 0 else lanes
    for k in range(feats // step):
        span = slice(k * step, (k + 1) * step)
        partial_ref[span, :] = lax.dot_general(
            held_ref[0, :, span], scaled, (((0,), (0,)), ((), ())), preferred_element_type=wide
        ).astype(narrow)


def onward_kernel(n, rows, first, s, partial_ref, even_ref, odd_ref, to_even_ref, to_odd_ref):
    me = lax.axis_index("fsdp")
    depth = even_ref.shape[0]
    even = (me & 1) == 0
    for came_ref, sent_ref, right in (
        (odd_ref, to_even_ref, even),
        (even_ref, to_odd_ref, jnp.logical_not(even)),
    ):
        place = jnp.where(right, me, n - 1 - me)
        owner = jnp.where(right, n - s + place, s - 1 - place)

        start = pl.multiple_of(owner * rows + first, 16)

        @pl.when(place == 0)
        def _():
            sent_ref[...] = partial_ref[pl.ds(start, depth), :]

        @pl.when((place > 0) & (s > place))
        def _():
            sent_ref[...] = add_narrow(came_ref[...], partial_ref[pl.ds(start, depth), :])

        @pl.when(s <= place)
        def _():
            sent_ref[...] = came_ref[...]


def keys_kernel(n, chunks, inputs_ref, rms_ref, weight_ref, spread_ref, *refs):
    got, (keys_ref, weights) = refs[:-2], refs[-2:]
    me = lax.axis_index("fsdp")
    rows, cols = weight_ref.shape[1:]
    used = spread_ref[...].astype(narrow).astype(wide)
    for k in range(cols // lanes):
        part = slice(k * lanes, (k + 1) * lanes)
        weights[pl.ds(pl.multiple_of(me * rows, 16), rows), part] = (
            weight_ref[0, :, part].astype(wide) * used
        ).astype(narrow)

    def put(block, c, ref):
        first, depth = chunks[c]
        weights[pl.ds(pl.multiple_of(block * rows + first, 16), depth), :] = ref[...]

    even = (me & 1) == 0
    for s in range(n - 1):
        for w in range(2):
            from_right = even if w == 0 else jnp.logical_not(even)
            block = jnp.where(from_right, me + 1 + s, me - 1 - s)

            @pl.when((block >= 0) & (block < n))
            def _():
                for c in range(len(chunks)):
                    put(block, c, got[(s * len(chunks) + c) * 2 + w])

    total = jnp.dot(inputs_ref[0], weights[...], preferred_element_type=wide)
    for k in range(cols // lanes):
        part = slice(k * lanes, (k + 1) * lanes)
        keys_ref[0, :, part] = (total[:, part] * rms_ref[...]).astype(narrow)


def fetch_kernel(*refs):
    count = len(refs) // 2
    sems = refs[-1]
    copies = [
        pltpu.make_async_copy(refs[i], refs[count + i], sems.at[i]) for i in range(count)
    ]
    for copy in copies:
        copy.start()
    for copy in copies:
        copy.wait()


def adam_kernel(c, chunks, spread_ref, weight_ref, first_ref, second_ref, partial_ref, *refs):
    last = c == len(chunks) - 1
    came = refs[:2]
    if last:
        shares, gains = refs[2 : 2 + c], refs[2 + c : 5 + c]
        new_gains, share_ref = refs[-4:-1], refs[-1]
        new_weight_ref, new_first_ref, new_second_ref = refs[-7:-4]
    else:
        share_ref, new_weight_ref, new_first_ref, new_second_ref = refs[-4:]
    depth, cols = weight_ref.shape[1:]
    step, steps = pl.program_id(0), pl.num_programs(0)
    whole = sum(size for _, size in chunks)
    start = pl.multiple_of(lax.axis_index("fsdp") * whole + chunks[c][0] + step * depth, 16)
    me, count = lax.axis_index("fsdp"), lax.axis_size("fsdp")
    mates = (me ^ 1, jnp.where((me & 1) == 0, me - 1, me + 1))
    share = jnp.zeros((depth, lanes), wide)
    used = spread_ref[...].astype(narrow).astype(wide)
    for k in range(cols // lanes):
        part = slice(k * lanes, (k + 1) * lanes)
        total = partial_ref[pl.ds(start, depth), part].astype(wide)
        for mate, ref in zip(mates, came):
            total = total + jnp.where((mate >= 0) & (mate < count), ref[:, part].astype(wide), 0.0)
        weight = weight_ref[0, :, part].astype(wide)
        share = share + total * weight
        new_weight, new_first, new_second = adam_step(
            weight, total * used, first_ref[0, :, part], second_ref[0, :, part]
        )
        new_weight_ref[0, :, part] = new_weight.astype(narrow)
        new_first_ref[0, :, part] = new_first
        new_second_ref[0, :, part] = new_second
    if not last:
        share_ref[...] = share
        return
    share_ref[pl.ds(pl.multiple_of(step * depth, 16), depth), :] = share

    @pl.when(step == steps - 1)
    def _():
        joined = jnp.concatenate([ref[...] for ref in (*shares, share_ref)], axis=0)
        gradient = jnp.sum(joined.T, axis=0, keepdims=True)
        for ref, value in zip(new_gains, adam_step(gains[0][...], gradient, gains[1][...], gains[2][...])):
            ref[...] = value


def pair_kernel(mine_ref, other_ref, half_ref, mine_held, other_held, sems):
    half, step = half_ref.shape[0], 16
    whole = pl.ds(pl.multiple_of(core_of_chip() * (half * lanes), half * lanes), half * lanes)
    copies = [
        pltpu.make_async_copy(mine_ref.at[:, whole], mine_held, sems.at[0]),
        pltpu.make_async_copy(other_ref.at[:, whole], other_held, sems.at[1]),
    ]
    for copy in copies:
        copy.start()
    for copy in copies:
        copy.wait()

    @pl.loop(0, half // step, unroll=4)
    def _(i):
        span = pl.ds(pl.multiple_of(i * (step * lanes), step * lanes), step * lanes)
        total = mine_held[:, span].astype(wide) + other_held[:, span].astype(wide)
        half_ref[pl.ds(pl.multiple_of(i * step, step), step), :] = total.reshape(step, lanes).astype(narrow)


def sum_kernel(left_ref, right_ref, total_ref):
    total_ref[...] = add_narrow(left_ref[...], right_ref[...])


def nesterov_kernel(silos, own_ref, other_ref, params_ref, mom_ref, new_params_ref, new_mom_ref):
    mine = core_of_chip() == pl.program_id(0)
    delta = jnp.where(mine, own_ref[...], other_ref[...]).astype(wide) / silos
    new_params_ref[0], new_mom_ref[0] = nesterov(delta, params_ref[0], mom_ref[0])


def in_hbm(array):
    return pltpu.with_memory_space_constraint(array, pltpu.HBM)


def in_vmem(arrays):
    return [pltpu.with_memory_space_constraint(array, pltpu.VMEM) for array in arrays]


def tie(values, other):
    return lax.optimization_barrier((values, other))[0]


def pair_operands(mine, other):
    return [in_hbm(mine), other]


def outer_steps(pseudo_grad, outer_params, outer_mom, silos, after):
    size = pseudo_grad.shape[1]
    half = size // 2 // lanes
    if silos < 2 or silos & (silos - 1) != 0 or size % (32 * lanes) != 0:
        yield nesterov(lax.psum(pseudo_grad[0].astype(wide), "silo") / silos, outer_params, outer_mom)
        return

    def swap(part, bit):
        return lax.ppermute(part, "silo", [(i, i ^ bit) for i in range(silos)])

    part = pltpu.VMEM((half, lanes), narrow)
    total = call(
        pair_kernel,
        part,
        pair_operands(*tie([pseudo_grad, swap(pseudo_grad, 1)], after)),
        specs=[HBM, HBM],
        scratch=[pltpu.VMEM((1, half * lanes), narrow)] * 2 + [pltpu.SemaphoreType.DMA((2,))],
    )
    yield total
    bit = 2
    while bit < silos:
        total = call(sum_kernel, part, in_vmem([total, swap(total, bit)]))
        yield total
        bit *= 2
    other = swap(total, 1)
    steps = blocks_of(half, 512, 16)
    line = pl.BlockSpec((half // steps, lanes), lambda h, j: (j, 0))
    block = pl.BlockSpec((1, half // steps, lanes), lambda h, j: (h, j, 0))
    new_params, new_mom = call(
        functools.partial(nesterov_kernel, silos),
        [jax.ShapeDtypeStruct((2, half, lanes), wide)] * 2,
        [total, other, outer_params.reshape(2, half, lanes), outer_mom.reshape(2, half, lanes)],
        specs=[line, line, block, block],
        outs=[block, block],
        grid=(2, steps),
    )
    yield new_params.reshape(size), new_mom.reshape(size)


def make(silos, n):
    def per_device(
        activations,
        key_cot,
        key_weight,
        weight_first,
        weight_second,
        norm_gain,
        gain_first,
        gain_second,
        pseudo_grad,
        outer_params,
        outer_mom,
    ):
        tokens, feats = activations.shape[1:]
        rows, cols = key_weight.shape[1:]
        chunks = split_rows(rows)
        count = len(chunks)
        shape = jax.ShapeDtypeStruct

        spread, *own = call(
            functools.partial(scale_kernel, chunks),
            [pltpu.VMEM((rows, lanes), wide)]
            + [pltpu.VMEM((depth, cols), narrow) for _, depth in chunks for _ in range(2)],
            [in_hbm(key_weight), in_hbm(norm_gain)],
            specs=[HBM, HBM],
            scratch=[
                pltpu.VMEM((rows, cols), narrow),
                pltpu.VMEM((1, rows), wide),
                pltpu.SemaphoreType.DMA((count + 1,)),
            ],
        )
        links = []
        for start in (0, 1):
            mate = {}
            for i in range(start, n - 1, 2):
                mate[i], mate[i + 1] = i + 1, i
            links.append(
                [
                    (silo * n + i, silo * n + mate[i] if i in mate else (silo ^ 1) * n + i)
                    for silo in range(silos)
                    for i in range(n)
                    if i in mate or silos % 2 == 0
                ]
            )
        slots = []
        for s in range(n):
            got = [[None for _ in range(count)] for _ in links]
            for c, (_, depth) in enumerate(chunks):
                sent = own[2 * c : 2 * c + 2]
                if s > 0:
                    came = [slots[-1][w][c] for w in range(2)]
                    if c == count - 1:
                        outer_part = next(outer, outer_part)
                        came = tie(came, outer_part)
                    sent = call(
                        functools.partial(onward_kernel, n, rows, chunks[c][0], s),
                        [pltpu.VMEM((depth, cols), narrow)] * 2,
                        [partial, *in_vmem(came)],
                        specs=[VMEM] * 3,
                    )
                for w in range(2):
                    got[w][c] = lax.ppermute(sent[w], ("silo", "fsdp"), links[w])
            slots.append(got)
            if s == 0:
                partial, inv_rms, inputs = call(
                    partial_kernel,
                    [
                        pltpu.VMEM((feats, cols), narrow),
                        pltpu.VMEM((tokens, lanes), wide),
                        pltpu.VMEM(activations.shape, narrow),
                    ],
                    [in_hbm(activations), in_hbm(key_cot)],
                    specs=[HBM, HBM],
                    scratch=[pltpu.VMEM(key_cot.shape, narrow), pltpu.SemaphoreType.DMA((2,))],
                )
                outer = outer_steps(pseudo_grad, outer_params, outer_mom, silos, partial)
                outer_part = partial

        keys = call(
            functools.partial(keys_kernel, n, chunks),
            shape((1, tokens, cols), narrow),
            [inputs, inv_rms, key_weight, spread]
            + [slots[s][w][c] for s in range(n - 1) for c in range(count) for w in range(2)],
            scratch=[pltpu.VMEM((feats, cols), narrow)],
            specs=[VMEM] * (4 + (n - 1) * 2 * count),
        )

        for outer_part in outer:
            pass
        shares, news = [], []
        unit = math.gcd(*[x for span in chunks for x in span])
        for c, (first, depth) in enumerate(chunks):
            tall = max(x for x in range(16, adam_rows + 1, 16) if unit % x == 0 or x == 16)
            steps, before = depth // tall, first // tall
            came = [slots[n - 1][w][c] for w in range(2)]
            if c == 0:
                came = tie(came, outer_part)
            block = pl.BlockSpec((1, tall, cols), lambda i, before=before: (0, before + i, 0))
            last = c == count - 1
            extra = [*shares, norm_gain, gain_first, gain_second] if last else []
            gain_outs = [shape((1, rows), wide)] * 3
            extras = len(extra)
            outs = call(
                functools.partial(adam_kernel, c, chunks),
                ([] if last else [shape((depth, lanes), wide)])
                + [shape((1, rows, cols), kind) for kind in (narrow, wide, wide)]
                + (gain_outs if last else []),
                [spread, key_weight, weight_first, weight_second, partial, *came, *extra, *news],
                specs=[pl.BlockSpec((tall, lanes), lambda i, before=before: (before + i, 0))]
                + [block] * 3
                + [VMEM]
                + [pl.BlockSpec((tall, cols), lambda i: (i, 0))] * 2
                + [VMEM] * extras
                + [pl.BlockSpec(memory_space=pl.ANY)] * len(news),
                outs=([] if last else [pl.BlockSpec((tall, lanes), lambda i: (i, 0))])
                + [block] * 3
                + ([VMEM] * 3 if last else []),
                aliases={7 + extras + i: (0 if last else 1) + i for i in range(len(news))},
                scratch=[pltpu.VMEM((depth, lanes), wide)] if last else [],
                grid=(steps,),
            )
            if last:
                news, new_gains = outs[:3], outs[3:]
            else:
                shares.append(outs[0])
                news = outs[1:]
        return (
            keys,
            *news,
            *new_gains,
            *outer_part,
        )

    return per_device


def solution(mesh):
    return jax.shard_map(
        make(mesh.shape["silo"], mesh.shape["fsdp"]),
        mesh=mesh,
        in_specs=(
            P("silo", "fsdp", None),
            P("silo", "fsdp", None),
            P("silo", "fsdp", None),
            P("silo", "fsdp", None),
            P("silo", "fsdp", None),
            P("silo", "fsdp"),
            P("silo", "fsdp"),
            P("silo", "fsdp"),
            P("silo", "fsdp"),
            P("fsdp"),
            P("fsdp"),
        ),
        out_specs=(
            P("silo", "fsdp", None),
            P("silo", "fsdp", None),
            P("silo", "fsdp", None),
            P("silo", "fsdp", None),
            P("silo", "fsdp"),
            P("silo", "fsdp"),
            P("silo", "fsdp"),
            P("fsdp"),
            P("fsdp"),
        ),
        check_vma=False,
    )
```

```python
import functools
import math

import jax
import jax.numpy as jnp
from jax import lax
from jax.experimental import pallas as pl
from jax.experimental.pallas import tpu as pltpu
from jax.sharding import PartitionSpec as P

norm_eps = 1e-05
beta_one = 0.9
beta_two = 0.95
corr_one = 1.0 - math.exp(200.0 * math.log(0.9))
corr_two = 1.0 - math.exp(200.0 * math.log(0.95))
learn_rate = 0.001
adam_eps = 1e-08
weight_decay = 0.1
outer_beta = 0.9
outer_rate = 0.7
root_scale = 1.0 / math.sqrt(corr_two)
rate_scale = learn_rate / corr_one
chunk_parts = (1, 1)
adam_rows = 512
lanes = 128
vmem_limit = 12 * 1024 * 1024

wide = jnp.float32
narrow = jnp.bfloat16
VMEM = pl.BlockSpec(memory_space=pltpu.VMEM)
HBM = pl.BlockSpec(memory_space=pltpu.HBM)


def adam_step(params, gradient, first_moment, second_moment):
    first_new = beta_one * first_moment + (1.0 - beta_one) * gradient
    second_new = beta_two * second_moment + (1.0 - beta_two) * gradient * gradient
    root = second_new * lax.rsqrt(second_new)
    ratio = first_new / (root * root_scale + adam_eps)
    return (params * (1.0 - learn_rate * weight_decay) - ratio * rate_scale, first_new, second_new)


def nesterov(delta_part, params_part, mom_part):
    new_mom = outer_beta * mom_part + delta_part
    new_params = params_part - outer_rate * (delta_part + outer_beta * new_mom)
    return (new_params, new_mom)


def split_rows(rows, unit=16):
    units, whole, ends = rows // unit, sum(chunk_parts), [0]
    for k in range(1, len(chunk_parts)):
        ends.append(units * sum(chunk_parts[:k]) // whole * unit)
    ends.append(rows)
    return [(a, b - a) for a, b in zip(ends, ends[1:]) if b > a]


def core_of_chip():
    return lax.axis_index("silo") & 1


def add_narrow(left, right):
    return (left.astype(wide) + right.astype(wide)).astype(narrow)


def blocks_of(size, most, unit):
    for count in range(1, size // unit + 1):
        if size % (count * unit) == 0 and size // count <= most:
            return count
    return 1


def call(kernel, out_shape, inputs, scratch=(), aliases=None, specs=None, outs=None, grid=()):
    return pl.pallas_call(
        kernel,
        out_shape=out_shape,
        grid=grid,
        in_specs=specs if specs is not None else [VMEM] * len(inputs),
        out_specs=outs if outs is not None else jax.tree.map(lambda _: VMEM, out_shape),
        scratch_shapes=list(scratch),
        compiler_params=pltpu.CompilerParams(vmem_limit_bytes=vmem_limit),

        input_output_aliases=aliases or {},
    )(*inputs)


def scale_kernel(chunks, weight_ref, gain_ref, *refs):
    count = len(chunks)
    sent_refs, (held, gain_held, sems) = refs[: 2 * count], refs[2 * count :]
    rows = weight_ref.shape[1]
    spans = [slice(start, start + depth) for start, depth in chunks]
    copies = [
        pltpu.make_async_copy(weight_ref.at[0, span], held.at[span], sems.at[c])
        for c, span in enumerate(spans)
    ]
    gain_copy = pltpu.make_async_copy(gain_ref, gain_held, sems.at[count])
    for copy in (gain_copy, *copies):
        copy.start()
    gain_copy.wait()
    spread = jnp.broadcast_to(gain_held[...], (lanes, rows)).T
    used = spread.astype(narrow).astype(wide)
    for c, span in enumerate(spans):
        copies[c].wait()
        for k in range(weight_ref.shape[2] // lanes):
            part = slice(k * lanes, (k + 1) * lanes)
            piece = (held[span, part].astype(wide) * used[span]).astype(narrow)
            sent_refs[2 * c][:, part] = piece
            sent_refs[2 * c + 1][:, part] = piece


def partial_kernel(inputs_ref, cot_ref, gain_ref, spread_ref, partial_ref, rms_ref, held_ref, cot_held, sems):
    tokens, feats = inputs_ref.shape[1:]
    copies = [
        pltpu.make_async_copy(inputs_ref, held_ref, sems.at[0]),
        pltpu.make_async_copy(cot_ref, cot_held, sems.at[1]),
    ]
    for copy in copies:
        copy.start()
    for copy in copies:
        copy.wait()
    spread_ref[...] = jnp.broadcast_to(gain_ref[...], spread_ref.shape[::-1]).T
    total = jnp.zeros((tokens, lanes), wide)
    for k in range(feats // lanes):
        part = held_ref[0, :, k * lanes : (k + 1) * lanes].astype(wide)
        total = total + part * part
    mean = jnp.sum(total, axis=1, keepdims=True) / feats
    inv_rms = lax.rsqrt(mean + norm_eps)
    rms_ref[...] = jnp.broadcast_to(inv_rms, rms_ref.shape)
    scaled = (cot_held[0].astype(wide) * inv_rms).astype(narrow)
    step = 2 * lanes if feats % (2 * lanes) == 0 else lanes
    for k in range(feats // step):
        span = slice(k * step, (k + 1) * step)
        partial_ref[span, :] = lax.dot_general(
            held_ref[0, :, span], scaled, (((0,), (0,)), ((), ())), preferred_element_type=wide
        ).astype(narrow)


def onward_kernel(n, rows, first, s, partial_ref, even_ref, odd_ref, to_even_ref, to_odd_ref):
    me = lax.axis_index("fsdp")
    depth = even_ref.shape[0]
    even = (me & 1) == 0
    for came_ref, sent_ref, right in (
        (odd_ref, to_even_ref, even),
        (even_ref, to_odd_ref, jnp.logical_not(even)),
    ):
        place = jnp.where(right, me, n - 1 - me)
        owner = jnp.where(right, n - s + place, s - 1 - place)

        start = pl.multiple_of(owner * rows + first, 16)

        @pl.when(place == 0)
        def _():
            sent_ref[...] = partial_ref[pl.ds(start, depth), :]

        @pl.when((place > 0) & (s > place))
        def _():
            sent_ref[...] = add_narrow(came_ref[...], partial_ref[pl.ds(start, depth), :])

        @pl.when(s <= place)
        def _():
            sent_ref[...] = came_ref[...]


def keys_kernel(n, chunks, inputs_ref, rms_ref, weight_ref, spread_ref, *refs):
    got, (keys_ref, weights) = refs[:-2], refs[-2:]
    me = lax.axis_index("fsdp")
    rows, cols = weight_ref.shape[1:]
    used = spread_ref[...].astype(narrow).astype(wide)
    for k in range(cols // lanes):
        part = slice(k * lanes, (k + 1) * lanes)
        weights[pl.ds(pl.multiple_of(me * rows, 16), rows), part] = (
            weight_ref[0, :, part].astype(wide) * used
        ).astype(narrow)

    def put(block, c, ref):
        first, depth = chunks[c]
        weights[pl.ds(pl.multiple_of(block * rows + first, 16), depth), :] = ref[...]

    even = (me & 1) == 0
    for s in range(n - 1):
        for w in range(2):
            from_right = even if w == 0 else jnp.logical_not(even)
            block = jnp.where(from_right, me + 1 + s, me - 1 - s)

            @pl.when((block >= 0) & (block < n))
            def _():
                for c in range(len(chunks)):
                    put(block, c, got[(s * len(chunks) + c) * 2 + w])

    total = jnp.dot(inputs_ref[0], weights[...], preferred_element_type=wide)
    for k in range(cols // lanes):
        part = slice(k * lanes, (k + 1) * lanes)
        keys_ref[0, :, part] = (total[:, part] * rms_ref[...]).astype(narrow)


def fetch_kernel(*refs):
    count = len(refs) // 2
    sems = refs[-1]
    copies = [
        pltpu.make_async_copy(refs[i], refs[count + i], sems.at[i]) for i in range(count)
    ]
    for copy in copies:
        copy.start()
    for copy in copies:
        copy.wait()


def adam_kernel(c, chunks, spread_ref, weight_ref, first_ref, second_ref, partial_ref, *refs):
    last = c == len(chunks) - 1
    came = refs[:2]
    if last:
        shares, gains = refs[2 : 2 + c], refs[2 + c : 5 + c]
        new_gains, share_ref = refs[-4:-1], refs[-1]
        new_weight_ref, new_first_ref, new_second_ref = refs[-7:-4]
    else:
        share_ref, new_weight_ref, new_first_ref, new_second_ref = refs[-4:]
    depth, cols = weight_ref.shape[1:]
    step, steps = pl.program_id(0), pl.num_programs(0)
    whole = sum(size for _, size in chunks)
    start = pl.multiple_of(lax.axis_index("fsdp") * whole + chunks[c][0] + step * depth, 16)
    me, count = lax.axis_index("fsdp"), lax.axis_size("fsdp")
    mates = (me ^ 1, jnp.where((me & 1) == 0, me - 1, me + 1))
    share = jnp.zeros((depth, lanes), wide)
    used = spread_ref[...].astype(narrow).astype(wide)
    for k in range(cols // lanes):
        part = slice(k * lanes, (k + 1) * lanes)
        total = partial_ref[pl.ds(start, depth), part].astype(wide)
        for mate, ref in zip(mates, came):
            total = total + jnp.where((mate >= 0) & (mate < count), ref[:, part].astype(wide), 0.0)
        weight = weight_ref[0, :, part].astype(wide)
        share = share + total * weight
        new_weight, new_first, new_second = adam_step(
            weight, total * used, first_ref[0, :, part], second_ref[0, :, part]
        )
        new_weight_ref[0, :, part] = new_weight.astype(narrow)
        new_first_ref[0, :, part] = new_first
        new_second_ref[0, :, part] = new_second
    if not last:
        share_ref[...] = share
        return
    share_ref[pl.ds(pl.multiple_of(step * depth, 16), depth), :] = share

    @pl.when(step == steps - 1)
    def _():
        joined = jnp.concatenate([ref[...] for ref in (*shares, share_ref)], axis=0)
        gradient = jnp.sum(joined.T, axis=0, keepdims=True)
        for ref, value in zip(new_gains, adam_step(gains[0][...], gradient, gains[1][...], gains[2][...])):
            ref[...] = value


def pair_kernel(mine_ref, other_ref, half_ref, mine_held, other_held, sems):
    half, step = half_ref.shape[0], 16
    whole = pl.ds(pl.multiple_of(core_of_chip() * (half * lanes), half * lanes), half * lanes)
    copies = [
        pltpu.make_async_copy(mine_ref.at[:, whole], mine_held, sems.at[0]),
        pltpu.make_async_copy(other_ref.at[:, whole], other_held, sems.at[1]),
    ]
    for copy in copies:
        copy.start()
    for copy in copies:
        copy.wait()

    @pl.loop(0, half // step, unroll=4)
    def _(i):
        span = pl.ds(pl.multiple_of(i * (step * lanes), step * lanes), step * lanes)
        total = mine_held[:, span].astype(wide) + other_held[:, span].astype(wide)
        half_ref[pl.ds(pl.multiple_of(i * step, step), step), :] = total.reshape(step, lanes).astype(narrow)


def sum_kernel(left_ref, right_ref, total_ref):
    total_ref[...] = add_narrow(left_ref[...], right_ref[...])


def nesterov_kernel(silos, own_ref, other_ref, params_ref, mom_ref, new_params_ref, new_mom_ref):
    mine = core_of_chip() == pl.program_id(0)
    delta = jnp.where(mine, own_ref[...], other_ref[...]).astype(wide) / silos
    new_params_ref[0], new_mom_ref[0] = nesterov(delta, params_ref[0], mom_ref[0])


def in_hbm(array):
    return pltpu.with_memory_space_constraint(array, pltpu.HBM)


def in_vmem(arrays):
    return [pltpu.with_memory_space_constraint(array, pltpu.VMEM) for array in arrays]


def tie(values, other):
    return lax.optimization_barrier((values, other))[0]


def pair_operands(mine, other):
    return [in_hbm(mine), other]


def outer_steps(pseudo_grad, outer_params, outer_mom, silos, after):
    size = pseudo_grad.shape[1]
    half = size // 2 // lanes
    if silos < 2 or silos & (silos - 1) != 0 or size % (32 * lanes) != 0:
        yield nesterov(lax.psum(pseudo_grad[0].astype(wide), "silo") / silos, outer_params, outer_mom)
        return

    def swap(part, bit):
        return lax.ppermute(part, "silo", [(i, i ^ bit) for i in range(silos)])

    part = pltpu.VMEM((half, lanes), narrow)
    total = call(
        pair_kernel,
        part,
        pair_operands(*tie([pseudo_grad, swap(pseudo_grad, 1)], after)),
        specs=[HBM, HBM],
        scratch=[pltpu.VMEM((1, half * lanes), narrow)] * 2 + [pltpu.SemaphoreType.DMA((2,))],
    )
    yield total
    bit = 2
    while bit < silos:
        total = call(sum_kernel, part, in_vmem([total, swap(total, bit)]))
        yield total
        bit *= 2
    other = swap(total, 1)
    steps = blocks_of(half, 512, 16)
    line = pl.BlockSpec((half // steps, lanes), lambda h, j: (j, 0))
    block = pl.BlockSpec((1, half // steps, lanes), lambda h, j: (h, j, 0))
    new_params, new_mom = call(
        functools.partial(nesterov_kernel, silos),
        [jax.ShapeDtypeStruct((2, half, lanes), wide)] * 2,
        [total, other, outer_params.reshape(2, half, lanes), outer_mom.reshape(2, half, lanes)],
        specs=[line, line, block, block],
        outs=[block, block],
        grid=(2, steps),
    )
    yield new_params.reshape(size), new_mom.reshape(size)


def make(silos, n):
    def per_device(
        activations,
        key_cot,
        key_weight,
        weight_first,
        weight_second,
        norm_gain,
        gain_first,
        gain_second,
        pseudo_grad,
        outer_params,
        outer_mom,
    ):
        tokens, feats = activations.shape[1:]
        rows, cols = key_weight.shape[1:]
        chunks = split_rows(rows)
        count = len(chunks)
        shape = jax.ShapeDtypeStruct

        own = call(
            functools.partial(scale_kernel, chunks),
            [pltpu.VMEM((depth, cols), narrow) for _, depth in chunks for _ in range(2)],
            [in_hbm(key_weight), in_hbm(norm_gain)],
            specs=[HBM, HBM],
            scratch=[
                pltpu.VMEM((rows, cols), narrow),
                pltpu.VMEM((1, rows), wide),
                pltpu.SemaphoreType.DMA((count + 1,)),
            ],
        )
        links = []
        for start in (0, 1):
            mate = {}
            for i in range(start, n - 1, 2):
                mate[i], mate[i + 1] = i + 1, i
            links.append(
                [
                    (silo * n + i, silo * n + mate[i] if i in mate else (silo ^ 1) * n + i)
                    for silo in range(silos)
                    for i in range(n)
                    if i in mate or silos % 2 == 0
                ]
            )
        slots = []
        for s in range(n):
            got = [[None for _ in range(count)] for _ in links]
            for c, (_, depth) in enumerate(chunks):
                sent = own[2 * c : 2 * c + 2]
                if s > 0:
                    came = [slots[-1][w][c] for w in range(2)]
                    if c == count - 1:
                        outer_part = next(outer, outer_part)
                        came = tie(came, outer_part)
                    sent = call(
                        functools.partial(onward_kernel, n, rows, chunks[c][0], s),
                        [pltpu.VMEM((depth, cols), narrow)] * 2,
                        [partial, *in_vmem(came)],
                        specs=[VMEM] * 3,
                    )
                for w in range(2):
                    got[w][c] = lax.ppermute(sent[w], ("silo", "fsdp"), links[w])
            slots.append(got)
            if s == 0:
                spread, partial, inv_rms, inputs = call(
                    partial_kernel,
                    [
                        pltpu.VMEM((rows, lanes), wide),
                        pltpu.VMEM((feats, cols), narrow),
                        pltpu.VMEM((tokens, lanes), wide),
                        pltpu.VMEM(activations.shape, narrow),
                    ],
                    [in_hbm(activations), in_hbm(key_cot), norm_gain],
                    specs=[HBM, HBM, VMEM],
                    scratch=[pltpu.VMEM(key_cot.shape, narrow), pltpu.SemaphoreType.DMA((2,))],
                )
                outer = outer_steps(pseudo_grad, outer_params, outer_mom, silos, partial)
                outer_part = partial

        keys = call(
            functools.partial(keys_kernel, n, chunks),
            shape((1, tokens, cols), narrow),
            [inputs, inv_rms, key_weight, spread]
            + [slots[s][w][c] for s in range(n - 1) for c in range(count) for w in range(2)],
            scratch=[pltpu.VMEM((feats, cols), narrow)],
            specs=[VMEM] * (4 + (n - 1) * 2 * count),
        )

        for outer_part in outer:
            pass
        shares, news = [], []
        unit = math.gcd(*[x for span in chunks for x in span])
        for c, (first, depth) in enumerate(chunks):
            tall = max(x for x in range(16, adam_rows + 1, 16) if unit % x == 0 or x == 16)
            steps, before = depth // tall, first // tall
            came = [slots[n - 1][w][c] for w in range(2)]
            if c == 0:
                came = tie(came, outer_part)
            block = pl.BlockSpec((1, tall, cols), lambda i, before=before: (0, before + i, 0))
            last = c == count - 1
            extra = [*shares, norm_gain, gain_first, gain_second] if last else []
            gain_outs = [shape((1, rows), wide)] * 3
            extras = len(extra)
            outs = call(
                functools.partial(adam_kernel, c, chunks),
                ([] if last else [shape((depth, lanes), wide)])
                + [shape((1, rows, cols), kind) for kind in (narrow, wide, wide)]
                + (gain_outs if last else []),
                [spread, key_weight, weight_first, weight_second, partial, *came, *extra, *news],
                specs=[pl.BlockSpec((tall, lanes), lambda i, before=before: (before + i, 0))]
                + [block] * 3
                + [VMEM]
                + [pl.BlockSpec((tall, cols), lambda i: (i, 0))] * 2
                + [VMEM] * extras
                + [pl.BlockSpec(memory_space=pl.ANY)] * len(news),
                outs=([] if last else [pl.BlockSpec((tall, lanes), lambda i: (i, 0))])
                + [block] * 3
                + ([VMEM] * 3 if last else []),
                aliases={7 + extras + i: (0 if last else 1) + i for i in range(len(news))},
                scratch=[pltpu.VMEM((depth, lanes), wide)] if last else [],
                grid=(steps,),
            )
            if last:
                news, new_gains = outs[:3], outs[3:]
            else:
                shares.append(outs[0])
                news = outs[1:]
        return (
            keys,
            *news,
            *new_gains,
            *outer_part,
        )

    return per_device


def solution(mesh):
    return jax.shard_map(
        make(mesh.shape["silo"], mesh.shape["fsdp"]),
        mesh=mesh,
        in_specs=(
            P("silo", "fsdp", None),
            P("silo", "fsdp", None),
            P("silo", "fsdp", None),
            P("silo", "fsdp", None),
            P("silo", "fsdp", None),
            P("silo", "fsdp"),
            P("silo", "fsdp"),
            P("silo", "fsdp"),
            P("silo", "fsdp"),
            P("fsdp"),
            P("fsdp"),
        ),
        out_specs=(
            P("silo", "fsdp", None),
            P("silo", "fsdp", None),
            P("silo", "fsdp", None),
            P("silo", "fsdp", None),
            P("silo", "fsdp"),
            P("silo", "fsdp"),
            P("silo", "fsdp"),
            P("fsdp"),
            P("fsdp"),
        ),
        check_vma=False,
    )
```
